32 devices in a mesh: gx: 4 (over y, core), gy: 8 (over z, x).
Axes of the slice: x: 2, y: 2, z: 4, core: 2. Of those that a mesh axis runs over, the one named last changes fastest.
Arguments:
- beta: float32 [16, 32, 1024], P(None, 'gx', 'gy'), may hold values from -6 to 6
- design: float32 [16, 16], replicated, may hold values from -1.5 to 1.5
- prior: float32 [16], replicated, may hold values from 0.25 to 4
- kept: int32 [16, 32, 1024], P(None, 'gx', 'gy'), may hold values from 1 to 40
- removed: int32 [16, 32, 1024], P(None, 'gx', 'gy'), may hold values from 0 to 8
- removed_labels: int32 [16, 32, 1024], P(None, 'gx', 'gy'), may hold values from 0 to 8, as said below
Outputs:
- newton_step: float32 [16, 32, 1024], P(None, 'gx', 'gy')
The draws below stay inside these ranges and needn't reach their ends.
Inputs may be any that keep to these rules, and one draw needn't show every extreme that they name: `removed_labels`: each entry is at most the entry of removed at the same place.
All inputs are finite; a program needn't handle non-finite values.
Results may differ from the reference program's by a relative error of at most 0.00022.
Values sent between devices are 32-bit elements; how exact they have to be, the bound alone decides.
No kernel may reach another device: no remote copies, remote signals or barrier semaphores. Data moves between devices by JAX's collectives and lax.ppermute only.
A program may use at most 64 MiB of HBM per device.

```python
import math
import jax
import jax.numpy as jnp
from jax import lax

K = 16
J = 16
ITERS = 4
SWEEPS = 2
LEVELS = 4
COARSE_SWEEPS = 4
NX = 32
NY = 1024


def removal_pair(key):
    first = jax.random.fold_in(key, 11)
    second = jax.random.fold_in(key, 12)
    counts = jax.random.randint(first, (J, NX, NY), 0, 9, dtype=jnp.int32)
    labels = jax.random.randint(second, (J, NX, NY), 0, 9, dtype=jnp.int32) % (counts + 1)
    return (counts, labels)


def draw_removed(key, part):
    return removal_pair(key)[0]


def draw_removed_labels(key, part):
    return removal_pair(key)[1]


def touch_ends(array, key, smallest, largest):
    extent = array.shape
    place = [jax.random.randint(jax.random.fold_in(key, axis), (), 0, extent[axis]) for axis in range(len(extent))]
    array = array.at[tuple(place)].set(smallest)
    longest = extent.index(max(extent))
    place[longest] = (place[longest] + 1) % extent[longest]
    return array.at[tuple(place)].set(largest)


def level_of(stream_key, dims, split, least, top_value):
    def one(position, blocks):
        steps = jax.random.uniform(jax.random.fold_in(jax.random.fold_in(stream_key, 6), position), (blocks,), jnp.float32, least / len(split), top_value / len(split))
        return jnp.repeat(jnp.exp(steps), dims[position] // blocks).reshape((-1,) + (1,) * (len(dims) - position - 1))

    gain = one(*split[0])
    for cut in split[1:]:
        gain = gain * one(*cut)
    return gain


def normal_values(own_key, dims, deviation, bound, shards=(), held_as=jnp.bfloat16):
    gain = level_of(own_key, dims, shards, -0.22, 0.18) if shards else 1.0
    values = jax.random.normal(own_key, dims, jnp.float32) * deviation * gain
    return jnp.minimum(jnp.maximum(values, -bound), bound).astype(held_as)


def setup_inputs(seed: int = 0) -> dict:
    keys = jax.random.split(jax.random.key(seed), 7)
    beta = normal_values(keys[0], (K, NX, NY), 1.0, 6.0, ((1, 4), (2, 8)), jnp.float32)
    design = normal_values(keys[1], (J, K), K ** -0.5, 1.5, (), jnp.float32)
    prior = jnp.clip(jnp.exp(jax.random.uniform(keys[2], (K,), jnp.float32, math.log(0.25), math.log(4.0))), 0.25, 4.0)
    kept = touch_ends(jax.random.randint(keys[3], (J, NX, NY), 1, 41), jax.random.fold_in(keys[3], 1), 1, 40).astype(jnp.int32)
    removed = draw_removed(jax.random.fold_in(keys[6], 71), 0)
    removed_labels = draw_removed_labels(jax.random.fold_in(keys[6], 71), 0)
    return {"beta": beta, "design": design, "prior": prior, "kept": kept, "removed": removed, "removed_labels": removed_labels}


damping = 0.7
highest = lax.Precision.HIGHEST


def gauss_jordan(blocks):
    size = blocks.shape[0]
    for pivot_at in range(size):
        pivots = blocks[pivot_at, pivot_at]
        scaled = blocks[pivot_at].at[pivot_at].set(1.0) / pivots[None]
        factors = blocks[:, pivot_at]
        blocks = blocks.at[:, pivot_at].set(0.0) - factors[:, None] * scaled[None]
        blocks = blocks.at[pivot_at].set(scaled)
    return blocks


def apply_inverse(inverse, vector):
    return jnp.einsum("klxy,lxy->kxy", inverse, vector, precision=highest)


def operate(field, padded, design, weights, prior, scale):
    inner = jnp.einsum("jk,kxy->jxy", design, field, precision=highest)
    data_term = jnp.einsum("jk,jxy->kxy", design, weights * inner, precision=highest)
    beside = padded[:, 2:, 1:-1] + padded[:, :-2, 1:-1] + padded[:, 1:-1, 2:] + padded[:, 1:-1, :-2]
    return data_term + scale * prior[:, None, None] * (4.0 * field - beside)


def restrict(field):
    chans, rows, cols = field.shape
    return field.reshape(chans, rows // 2, 2, cols // 2, 2).sum(axis=(2, 4))


def prolong(field):
    return jnp.repeat(jnp.repeat(field, 2, axis=1), 2, axis=2)


def build_inverse(design, weights, prior, scale):
    outer = design[:, :, None] * design[:, None, :]
    blocks = jnp.einsum("jkl,jxy->klxy", outer, weights, precision=highest)
    blocks = blocks + (4.0 * scale * jnp.diag(prior))[:, :, None, None]
    return gauss_jordan(blocks)


def zero_pad(field):
    return jnp.pad(field, ((0, 0), (1, 1), (1, 1)))


def smooth(field, rhs, design, weights, inverse, prior, scale):
    leftover = rhs - operate(field, zero_pad(field), design, weights, prior, scale)
    return field + damping * apply_inverse(inverse, leftover)


def sweeps(rhs, count, design, weights, inverse, prior, scale):
    field = damping * apply_inverse(inverse, rhs)
    for sweep in range(count - 1):
        field = smooth(field, rhs, design, weights, inverse, prior, scale)
    return field


def multigrid(rhs, level, tables, design, prior):
    weights, inverse = tables[level]
    scale = 2.0 ** level
    if level == len(tables) - 1:
        return sweeps(rhs, COARSE_SWEEPS, design, weights, inverse, prior, scale)
    field = sweeps(rhs, SWEEPS, design, weights, inverse, prior, scale)
    leftover = rhs - operate(field, zero_pad(field), design, weights, prior, scale)
    field = field + prolong(multigrid(restrict(leftover), level + 1, tables, design, prior))
    for sweep in range(SWEEPS):
        field = smooth(field, rhs, design, weights, inverse, prior, scale)
    return field


def reference(beta, design, prior, kept, removed, removed_labels):
    logits = jnp.einsum("jk,kxy->jxy", design, beta, precision=highest)
    prob = 1.0 / (1.0 + jnp.exp(-logits))
    weights = kept.astype(jnp.float32) * prob * (1.0 - prob)
    source = removed.astype(jnp.float32) * prob - removed_labels.astype(jnp.float32)
    rhs = jnp.einsum("jk,jxy->kxy", design, source, precision=highest)
    tables = []
    for level in range(LEVELS):
        if level > 0:
            weights = restrict(weights)
        tables.append((weights, build_inverse(design, weights, prior, 2.0 ** level)))
    fine_weights = tables[0][0]
    newton_step = jnp.zeros_like(rhs)
    residual = rhs
    precond = multigrid(residual, 0, tables, design, prior)
    direction = precond
    gamma = jnp.sum(residual * precond)
    for step in range(ITERS):
        image = operate(direction, zero_pad(direction), design, fine_weights, prior, 1.0)
        alpha = gamma / jnp.sum(direction * image)
        newton_step = newton_step + alpha * direction
        residual = residual - alpha * image
        if step + 1 < ITERS:
            precond = multigrid(residual, 0, tables, design, prior)
            gamma_next = jnp.sum(residual * precond)
            direction = precond + (gamma_next / gamma) * direction
            gamma = gamma_next
    return newton_step
```

```python
import functools

import jax
import jax.numpy as jnp
from jax import lax
from jax.experimental import pallas as pl
from jax.experimental.pallas import tpu as pltpu
from jax.sharding import PartitionSpec as P

ITERS = 4
LEVELS = 4
COARSE_SWEEPS = 4
K = 16
BLOCK = 8
SEGMENT = 32
HALO = 8
OWN = 16
DAMPING = 0.7

highest = lax.Precision.HIGHEST
f32 = jnp.float32

SIDES = [BLOCK >> m for m in range(LEVELS)]
COUNTS = [n * n for n in SIDES]
OFFSETS = [sum(COUNTS[:m]) for m in range(LEVELS)]
SLOTS = -(-sum(COUNTS) // 8) * 8
SPLITS = ((0, 0), (0, 1), (0, 2), (1, 0), (1, 1), (2, 0))

VMEM = pl.BlockSpec(memory_space=pltpu.VMEM)
SMEM = pl.BlockSpec(memory_space=pltpu.SMEM)


def params(mib):
    return pltpu.CompilerParams(vmem_limit_bytes=mib << 20)


def lanes_of(shape):
    return lax.broadcasted_iota(jnp.int32, shape, len(shape) - 1)


def roll(x, shift):
    shift = shift % x.shape[-1]
    return x if shift == 0 else pltpu.roll(x, shift, x.ndim - 1)


def lane_order():
    row = lax.broadcasted_iota(jnp.int32, (128, 128), 0)
    lane = lax.broadcasted_iota(jnp.int32, (128, 128), 1)
    return (lane == (row % BLOCK) * OWN + row // BLOCK).astype(f32)


def prepare_kernel(place, design, beta, kept, removed, labels, own, edge_a, edge_b, tile):
    probs = []
    for j in range(K):
        logit = sum(design[j, k] * beta[k] for k in range(K))
        prob = 1.0 / (1.0 + jnp.exp(-logit))
        probs.append(removed[j].astype(f32) * prob - labels[j].astype(f32))
        tile[pl.ds(j * BLOCK, BLOCK), :] = kept[j].astype(f32) * prob * (1.0 - prob)
    for k in range(K):
        tile[pl.ds((K + k) * BLOCK, BLOCK), :] = sum(design[j, k] * probs[j] for j in range(K))
    tile[...] = jnp.dot(tile[...], lane_order(), precision=highest, preferred_element_type=f32)
    even = place[1] % 2 == 0
    low = lanes_of((K, 128)) % OWN < HALO
    for f in range(2):
        rows = [tile[pl.ds(f * K * BLOCK + t, K, stride=BLOCK), :] for t in range(BLOCK)]
        for t in range(BLOCK):
            own[f, t] = rows[t]
        for i in range(BLOCK // 2):
            left = jnp.where(low, rows[2 * i], roll(rows[2 * i + 1], HALO))
            right = jnp.where(low, roll(rows[2 * i], -HALO), rows[2 * i + 1])
            edge_a[f, i] = jnp.where(even, right, left)
            edge_b[f, i] = jnp.where(even, left, right)


def symmetric_inverse(a, n):
    a = dict(a)
    for p in range(n):
        d = 1.0 / a[p, p]
        col = {i: a[max(i, p), min(i, p)] for i in range(n) if i != p}
        fac = {i: col[i] * d for i in col}
        for i in col:
            for j in col:
                if j <= i:
                    a[i, j] = a[i, j] - fac[i] * col[j]
        for i in col:
            a[max(i, p), min(i, p)] = fac[i]
        a[p, p] = -d
    return {ij: -x for ij, x in a.items()}


def setup_kernel(place, prior, outer, g_own, g_edge, blocks, inverse, rhs, weights, pieces, coarse_blocks, work):
    width = rhs.shape[-1]
    groups = width // 128
    lane = lanes_of((K, 128))
    left_at = (place[1] + 1) % 2
    right_at = 1 - left_at
    for f, target in ((0, weights), (1, rhs)):
        for group in range(groups):
            for t in range(BLOCK):
                for s in range(BLOCK):
                    value = jnp.zeros((K, 128), f32)
                    for p in range(4):
                        at = group * 4 + p
                        base = p * SEGMENT
                        odd = (t % 2) * HALO
                        mid = roll(g_own[at, f, t], base + HALO - s * OWN)
                        low = roll(g_edge[at, left_at, f, t // 2], base - s * OWN - odd)
                        high = roll(g_edge[at, right_at, f, t // 2], base + SEGMENT - HALO - s * OWN - odd)
                        value = jnp.where((lane >= base) & (lane < base + HALO), low, value)
                        value = jnp.where((lane >= base + HALO) & (lane < base + HALO + OWN), mid, value)
                        value = jnp.where((lane >= base + HALO + OWN) & (lane < base + SEGMENT), high, value)
                    target[s * BLOCK + t, :, pl.ds(group * 128, 128)] = value
    for m in range(1, LEVELS):
        n, fine, coarse = SIDES[m], OFFSETS[m - 1], OFFSETS[m]
        for s in range(n):
            for t in range(n):
                corner = fine + (2 * s) * (2 * n) + 2 * t
                weights[coarse + s * n + t] = (
                    weights[corner] + weights[corner + 1] + weights[corner + 2 * n] + weights[corner + 2 * n + 1]
                )
    for slot in range(sum(COUNTS), SLOTS):
        weights[slot] = jnp.zeros((K, width), f32)

    def split(slot, carry):
        for group in range(groups):
            rest = weights[slot, :, pl.ds(group * 128, 128)]
            parts = []
            for _ in range(3):
                part = rest.astype(jnp.bfloat16)
                parts.append(part)
                rest = rest - part.astype(f32)
            for i, (_, b) in enumerate(SPLITS):
                pieces[group, slot, pl.ds(i * K, K), :] = parts[b]
        return carry

    lax.fori_loop(0, SLOTS, split, 0)

    tables = ((blocks, 0, COUNTS[0]), (coarse_blocks, COUNTS[0], SLOTS - COUNTS[0]))
    for table, first, count in tables:

        def multiply(step, carry, table=table, first=first):
            for group in range(groups):
                for i in range(4):
                    slot = step * 4 + i
                    table[group, slot] = jnp.dot(
                        outer[...], pieces[group, first + slot], preferred_element_type=f32
                    )
            return carry

        lax.fori_loop(0, count // 4, multiply, 0)

    flat_inverse = inverse.reshape(groups * SLOTS * K * K, 128)
    column = lanes_of((8, 128)) % SEGMENT
    inside = ((place[1] > 0) | (column >= HALO)) & ((place[1] < place[2] - 1) | (column < HALO + OWN))
    damped = jnp.where(inside, DAMPING, 0.0).astype(f32)
    half = K // 2

    for group, (table, offset, count) in ((x, y) for x in range(groups) for y in tables):
        flat_blocks = table.reshape(groups * count * K * K, 128)

        def invert(g, carry, group=group, flat_blocks=flat_blocks, offset=offset, count=count):
            slot = offset + g * 8 + lax.broadcasted_iota(jnp.int32, (8, 128), 0)
            scale = jnp.where(
                slot < OFFSETS[1], 4.0, jnp.where(slot < OFFSETS[2], 8.0, jnp.where(slot < OFFSETS[3], 16.0, 32.0))
            ).astype(f32)
            source = (group * count + g * 8) * (K * K)
            target = (group * SLOTS + offset + g * 8) * (K * K)

            def load(k, l):
                value = flat_blocks[pl.ds(source + l * K + k, 8, stride=K * K), :]
                return value + scale * prior[k] if k == l else value

            def store(k, l, value):
                value = value * damped
                flat_inverse[pl.ds(target + l * K + k, 8, stride=K * K), :] = value
                if k != l:
                    flat_inverse[pl.ds(target + k * K + l, 8, stride=K * K), :] = value

            first = symmetric_inverse({(i, j): load(i, j) for i in range(half) for j in range(i + 1)}, half)
            for i in range(half):
                for j in range(half):
                    work[0, i * half + j] = load(half + j, i)
            for j in range(half):
                b = [work[0, i * half + j] for i in range(half)]
                for i in range(half):
                    work[1, i * half + j] = sum(first[max(i, h), min(i, h)] * b[h] for h in range(half))
            schur = {(i, j): load(half + i, half + j) for i in range(half) for j in range(i + 1)}
            for h in range(half):
                b = [work[0, h * half + j] for j in range(half)]
                y = [work[1, h * half + j] for j in range(half)]
                for i in range(half):
                    for j in range(i + 1):
                        schur[i, j] = schur[i, j] - b[i] * y[j]
            second = symmetric_inverse(schur, half)
            for (i, j), value in second.items():
                store(half + i, half + j, value)
            for i in range(half):
                y = [work[1, i * half + j] for j in range(half)]
                for j in range(half):
                    z = sum(y[h] * second[max(h, j), min(h, j)] for h in range(half))
                    work[0, i * half + j] = z
                    store(half + j, i, -z)
            for h in range(half):
                z = [work[0, i * half + h] for i in range(half)]
                y = [work[1, i * half + h] for i in range(half)]
                for i in range(half):
                    for j in range(i + 1):
                        first[i, j] = first[i, j] + z[i] * y[j]
            for (i, j), value in first.items():
                store(i, j, value)
            return carry

        lax.fori_loop(0, count // 8, invert, 0)


def beside(read, m, s, t, above, below):
    n = SIDES[m]
    total = read(s - 1, t) if s > 0 else roll(read(n - 1, t), 1)
    total = total + (read(s + 1, t) if s < n - 1 else roll(read(0, t), -1))
    total = total + (read(s, t - 1) if t > 0 else jnp.where(above, roll(read(s, n - 1), SEGMENT), 0.0))
    return total + (read(s, t + 1) if t < n - 1 else jnp.where(below, roll(read(s, 0), -SEGMENT), 0.0))


def block_product(table, first, count, source, finish):
    def one(i, carry):
        for group in range(table.shape[0]):
            cols = pl.ds(group * 128, 128)
            total = None
            for l in range(K):
                term = table[group, first + i, pl.ds(l * K, K), :] * source[i, pl.ds(l, 1), cols]
                total = term if total is None else total + term
            finish(i, cols, total)
        return carry

    lax.fori_loop(0, count, one, 0, unroll=min(count, 8))


def v_cycle(inverse, prior, b, v, d, w):
    width = b[0].shape[-1]
    lane = lanes_of((K, width))
    above, below = lane >= SEGMENT, lane < width - SEGMENT
    weight = [jnp.broadcast_to(prior[...] * 2.0**m, (K, width)) for m in range(LEVELS)]

    def sweep(m, keep=None):
        n = SIDES[m]
        for s in range(n):
            for t in range(n):
                near = beside(lambda x, y: v[m][x * n + y], m, s, t, above, below)
                w[m][s * n + t] = b[m][s * n + t] + weight[m] * near

        def finish(i, cols, total):
            old = v[m][i, :, cols]
            v[m][i, :, cols] = 0.3 * old + total
            if keep is not None:
                keep[i, :, cols] = total - 0.4 * old

        block_product(inverse, OFFSETS[m], COUNTS[m], w[m], finish)

    def begin(m):
        def finish(i, cols, total):
            v[m][i, :, cols] = total

        block_product(inverse, OFFSETS[m], COUNTS[m], b[m], finish)

    for m in range(LEVELS - 1):
        n = SIDES[m]
        begin(m)
        sweep(m, d[m])
        for s in range(0, n, 2):
            for t in range(0, n, 2):
                near, own = None, None
                for x, y in ((s, t), (s, t + 1), (s + 1, t), (s + 1, t + 1)):
                    one = beside(lambda x, y: d[m][x * n + y], m, x, y, above, below)
                    near = one if near is None else near + one
                    one = b[m][x * n + y]
                    own = one if own is None else own + one
                b[m + 1][(s // 2) * (n // 2) + t // 2] = 0.09 * own + weight[m] * near
    begin(LEVELS - 1)
    for _ in range(COARSE_SWEEPS - 1):
        sweep(LEVELS - 1)
    for m in range(LEVELS - 2, -1, -1):
        n = SIDES[m]
        for s in range(n):
            for t in range(n):
                v[m][s * n + t] = v[m][s * n + t] + v[m + 1][(s // 2) * (n // 2) + t // 2]
        sweep(m)
        sweep(m)


def iterate_kernel(step, last, *refs):
    refs = list(refs)
    place, prior, blocks, inverse, residual_in = (refs.pop(0) for _ in range(5))
    if step > 0:
        sums, edge_a, edge_b, z_in, az_in = (refs.pop(0) for _ in range(5))
    if step > 1:
        old, x_in, p_in, ap_in = (refs.pop(0) for _ in range(4))
    z_out, az_out, parts = (refs.pop(0) for _ in range(3))
    if not last:
        send_a, send_b = (refs.pop(0) for _ in range(2))
    if step > 0:
        scalars, residual, x, p, ap = (refs.pop(0) for _ in range(5))
    b, v, d, w = (refs[i * LEVELS : (i + 1) * LEVELS] for i in range(4))
    width = z_out.shape[-1]
    lane = lanes_of((K, width))
    column = lane % SEGMENT
    mine = (column >= HALO) & (column < HALO + OWN)
    even = place[1] % 2 == 0
    count = COUNTS[0]
    if step > 0:
        gamma, alpha, beta, energy = coefficients(sums, old if step > 1 else None)
        scalars[...] = jnp.concatenate(
            [jnp.broadcast_to(gamma, (1, 128)), jnp.broadcast_to(energy, (1, 128)), jnp.zeros((6, 128), f32)], axis=0
        )
        left_side, right_side = column < HALO, column >= HALO + OWN
        for i in range(count // 4):
            left = jnp.where(even, edge_b[i], edge_a[i])
            right = jnp.where(even, edge_a[i], edge_b[i])
            for g in range(4):
                at = 4 * i + g
                image = jnp.where(left_side, roll(left, -HALO * g), az_in[at])
                image = jnp.where(right_side, roll(right, SEGMENT - HALO - HALO * g), image)
                direction = z_in[at]
                if step > 1:
                    direction = direction + beta * p_in[at]
                    image = image + beta * ap_in[at]
                p[at] = direction
                ap[at] = image
                x[at] = x_in[at] + alpha * direction if step > 1 else alpha * direction
                left_over = residual_in[at] - alpha * image
                residual[at] = left_over
                b[0][at] = left_over
    else:
        for at in range(count):
            b[0][at] = residual_in[at]

    v_cycle(inverse, prior, b, v, d, w)

    above, below = lane >= SEGMENT, lane < width - SEGMENT
    weight = jnp.broadcast_to(prior[...], (K, width))
    n = SIDES[0]
    for s in range(n):
        for t in range(n):
            near = beside(lambda x, y: v[0][x * n + y], 0, s, t, above, below)
            w[0][s * n + t] = weight * (4.0 * v[0][s * n + t] - near)

    def finish(i, cols, total):
        az_out[i, :, cols] = total + w[0][i, :, cols]
        z_out[i, :, cols] = v[0][i, :, cols]

    block_product(blocks, 0, count, v[0], finish)

    names = 3 if step > 0 else 2
    totals = [jnp.zeros((K, width), f32) for _ in range(names)]
    for at in range(count):
        z = z_out[at]
        totals[0] = totals[0] + z * b[0][at]
        totals[1] = totals[1] + z * az_out[at]
        if step > 0:
            totals[2] = totals[2] + z * ap[at]
    rows = []
    for total in totals:
        total = jnp.sum(jnp.where(mine, total, 0.0), axis=0, keepdims=True)
        rows.append(sum(total[:, g * 128 : (g + 1) * 128] for g in range(width // 128)))
    rows.append(jnp.zeros((8 - names, 128), f32))
    tile = jnp.concatenate(rows, axis=0)
    for i in range(parts.shape[0]):
        parts[i] = tile
    if not last:
        for i in range(count // 4):
            left, right = None, None
            for g in range(4):
                value = az_out[4 * i + g]
                low, high = roll(value, HALO * g - HALO), roll(value, HALO * g - OWN)
                here = (column >= HALO * g) & (column < HALO * g + HALO)
                left = low if left is None else jnp.where(here, low, left)
                right = high if right is None else jnp.where(here, high, right)
            send_a[i] = jnp.where(even, right, left)
            send_b[i] = jnp.where(even, left, right)


def coefficients(sums, old):
    total = sums[0]
    for i in range(1, sums.shape[0]):
        total = total + sums[i]
    total = jnp.sum(total, axis=1, keepdims=True)
    gamma, energy = total[0:1], total[1:2]
    beta = None
    if old is not None:
        beta = gamma / old[0:1, 0:1]
        energy = energy + beta * (2.0 * total[2:3] + beta * old[1:2, 0:1])
    return gamma, gamma / energy, beta, energy


def finish_kernel(place, sums, old, x, p, z, out, tile):
    _, alpha, beta, _ = coefficients(sums, old)
    group = pl.ds(pl.multiple_of((place[0] // 4) * 128, 128), 128)
    base = (place[0] % 4) * SEGMENT + HALO
    lane = lanes_of((K, 128))
    for t in range(BLOCK):
        packed = None
        for s in range(BLOCK):
            at = s * BLOCK + t
            value = x[at, :, group] + alpha * (z[at, :, group] + beta * p[at, :, group])
            value = pltpu.roll(value, (128 + s * OWN - base) % 128, 1)
            packed = value if packed is None else jnp.where(lane >= s * OWN, value, packed)
        tile[pl.ds(t, K, stride=BLOCK), :] = packed
    back = lax.dot_general(
        tile[...], lane_order(), (((1,), (1,)), ((), ())), precision=highest, preferred_element_type=f32
    )
    out[...] = back.reshape(K, BLOCK, 128)


def local(beta, design, prior, kept, removed, removed_labels):
    rows, cols = lax.axis_size("gx"), lax.axis_size("gy")
    width = rows * SEGMENT
    place = jnp.stack([lax.axis_index("gx"), lax.axis_index("gy"), jnp.int32(cols)]).astype(jnp.int32)
    pairs = [(i, i ^ 1) for i in range(cols)]
    others = [(0, 0)] + [(i, ((i + 1) ^ 1) - 1) for i in range(1, cols - 1)] + [(cols - 1, cols - 1)]
    others = others[1:-1]

    def shape(*dims, dtype=f32):
        return jax.ShapeDtypeStruct(dims, dtype)

    own, edge_a, edge_b = pl.pallas_call(
        prepare_kernel,
        out_shape=[shape(2, 8, K, 128), shape(2, 4, K, 128), shape(2, 4, K, 128)],
        in_specs=[SMEM, SMEM] + [VMEM] * 4,
        out_specs=[VMEM] * 3,
        scratch_shapes=[pltpu.VMEM((2 * K * BLOCK, 128), f32)],
        name="prepare",
    )(place, design, beta, kept, removed, removed_labels)
    edge_a = lax.ppermute(edge_a, "gy", pairs)
    edge_b = lax.ppermute(edge_b, "gy", others)
    g_own = lax.all_gather(own, "gx")
    g_edge = lax.all_gather(jnp.stack([edge_a, edge_b]), "gx")

    products = (design[:, :, None] * design[:, None, :]).reshape(K, K * K).T
    parts, rest = [], products
    for _ in range(3):
        part = lax.reduce_precision(rest, 8, 7)
        parts.append(part)
        rest = rest - part
    outer = jnp.concatenate([parts[a] for a, _ in SPLITS], axis=1).astype(jnp.bfloat16)
    prior_rows = prior[:, None]

    field = shape(COUNTS[0], K, width)
    blocks, inverse, residual = pl.pallas_call(
        setup_kernel,
        out_shape=[shape(width // 128, n, K * K, 128) for n in (COUNTS[0], SLOTS)] + [field],
        in_specs=[SMEM, SMEM] + [VMEM] * 3,
        out_specs=[VMEM] * 3,
        scratch_shapes=[
            pltpu.VMEM((SLOTS, K, width), f32),
            pltpu.VMEM((width // 128, SLOTS, len(SPLITS) * K, 128), jnp.bfloat16),
            pltpu.VMEM((width // 128, SLOTS - COUNTS[0], K * K, 128), f32),
            pltpu.VMEM((2, K * K // 4, 8, 128), f32),
        ],
        compiler_params=params(24 if width == 128 else 60),
        name="setup",
    )(place, prior, outer, g_own, g_edge)

    levels = [pltpu.VMEM((n, K, width), f32) for n in COUNTS]
    state = ()
    for step in range(ITERS):
        last = step == ITERS - 1
        operands = (place, prior_rows, blocks, inverse, residual) + state
        shapes = [field, field, shape(cols, 8, 128)]
        if not last:
            shapes += [shape(COUNTS[0] // 4, K, width)] * 2
        if step > 0:
            shapes += [shape(8, 128), field, field, field, field]
        outs = pl.pallas_call(
            functools.partial(iterate_kernel, step, last),
            out_shape=shapes,
            in_specs=[SMEM] + [VMEM] * (len(operands) - 1),
            out_specs=[VMEM] * len(shapes),
            scratch_shapes=levels * 4,
            compiler_params=params(24 if width == 128 else 60),
            name=f"iterate_{step}",
        )(*operands)
        z, az, sums = outs[:3]
        outs = outs[3:]
        sums = lax.all_to_all(sums, "gy", 0, 0, tiled=True)
        if not last:
            edge_a = lax.ppermute(outs[0], "gy", pairs)
            edge_b = lax.ppermute(outs[1], "gy", others)
            outs = outs[2:]
        history = ()
        if step > 0:
            scalars, residual, x, p, ap = outs
            history = (scalars, x, p, ap)
        if not last:
            state = (sums, edge_a, edge_b, z, az) + history
    return pl.pallas_call(
        finish_kernel,
        out_shape=shape(*beta.shape),
        in_specs=[SMEM] + [VMEM] * 5,
        out_specs=VMEM,
        scratch_shapes=[pltpu.VMEM((K * BLOCK, 128), f32)],
        name="finish",
    )(place, sums, scalars, x, p, z)


def solution(mesh):
    placed = (
        P(None, "gx", "gy"),
        P(),
        P(),
        P(None, "gx", "gy"),
        P(None, "gx", "gy"),
        P(None, "gx", "gy"),
    )
    return jax.shard_map(
        local, mesh=mesh, in_specs=placed, out_specs=P(None, "gx", "gy"), check_vma=False
    )
```

```python
import functools

import jax
import jax.numpy as jnp
from jax import lax
from jax.experimental import pallas as pl
from jax.experimental.pallas import tpu as pltpu
from jax.sharding import PartitionSpec as P

ITERS = 4
LEVELS = 4
COARSE_SWEEPS = 4
K = 16
BLOCK = 8
SEGMENT = 32
HALO = 8
OWN = 16
DAMPING = 0.7

highest = lax.Precision.HIGHEST
f32 = jnp.float32

SIDES = [BLOCK >> m for m in range(LEVELS)]
COUNTS = [n * n for n in SIDES]
OFFSETS = [sum(COUNTS[:m]) for m in range(LEVELS)]
SLOTS = -(-sum(COUNTS) // 8) * 8
ROWS = K * K + 8
SPLITS = ((0, 0), (0, 1), (0, 2), (1, 0), (1, 1), (2, 0))

VMEM = pl.BlockSpec(memory_space=pltpu.VMEM)
SMEM = pl.BlockSpec(memory_space=pltpu.SMEM)


def params(mib):
    return pltpu.CompilerParams(vmem_limit_bytes=mib << 20)


def lanes_of(shape):
    return lax.broadcasted_iota(jnp.int32, shape, len(shape) - 1)


def roll(x, shift):
    shift = shift % x.shape[-1]
    return x if shift == 0 else pltpu.roll(x, shift, x.ndim - 1)


def lane_order():
    row = lax.broadcasted_iota(jnp.int32, (128, 128), 0)
    lane = lax.broadcasted_iota(jnp.int32, (128, 128), 1)
    return (lane == (row % BLOCK) * OWN + row // BLOCK).astype(f32)


def prepare_kernel(place, design, beta, kept, removed, labels, own, edge_a, edge_b, tile):
    probs = []
    for j in range(K):
        logit = sum(design[j, k] * beta[k] for k in range(K))
        prob = 1.0 / (1.0 + jnp.exp(-logit))
        probs.append(removed[j].astype(f32) * prob - labels[j].astype(f32))
        tile[pl.ds(j * BLOCK, BLOCK), :] = kept[j].astype(f32) * prob * (1.0 - prob)
    for k in range(K):
        tile[pl.ds((K + k) * BLOCK, BLOCK), :] = sum(design[j, k] * probs[j] for j in range(K))
    tile[...] = jnp.dot(tile[...], lane_order(), precision=highest, preferred_element_type=f32)
    even = place[1] % 2 == 0
    low = lanes_of((K, 128)) % OWN < HALO
    for f in range(2):
        rows = [tile[pl.ds(f * K * BLOCK + t, K, stride=BLOCK), :] for t in range(BLOCK)]
        for t in range(BLOCK):
            own[f, t] = rows[t]
        for i in range(BLOCK // 2):
            left = jnp.where(low, rows[2 * i], roll(rows[2 * i + 1], HALO))
            right = jnp.where(low, roll(rows[2 * i], -HALO), rows[2 * i + 1])
            edge_a[f, i] = jnp.where(even, right, left)
            edge_b[f, i] = jnp.where(even, left, right)


def symmetric_inverse(a, n):
    a = dict(a)
    for p in range(n):
        d = 1.0 / a[p, p]
        col = {i: a[max(i, p), min(i, p)] for i in range(n) if i != p}
        fac = {i: col[i] * d for i in col}
        for i in col:
            for j in col:
                if j <= i:
                    a[i, j] = a[i, j] - fac[i] * col[j]
        for i in col:
            a[max(i, p), min(i, p)] = fac[i]
        a[p, p] = -d
    return {ij: -x for ij, x in a.items()}


def setup_kernel(place, prior, outer, *refs):
    rows = (len(refs) - 7) // 3
    g_own, g_left, g_right = (refs[i * rows : (i + 1) * rows] for i in range(3))
    blocks, inverse, rhs, weights, pieces, coarse_blocks, work = refs[3 * rows :]
    width = rhs.shape[-1]
    groups = width // 128
    lane = lanes_of((K, 128))
    even = place[1] % 2 == 0

    def store_pieces(slot, group, rest):
        cols = pl.ds((slot % 2) * 128, 128)
        parts = []
        for _ in range(3):
            part = rest.astype(jnp.bfloat16)
            parts.append(part)
            rest = rest - part.astype(f32)
        for i, (_, b) in enumerate(SPLITS):
            pieces[group, slot // 2, pl.ds(i * K, K), cols] = parts[b]

    for group in range(groups):
        bases = [(place[0] ^ o) * SEGMENT - group * 128 for o in range(rows)]
        masks = []
        for base in bases:
            at = lane - base
            masks.append(((at >= 0) & (at < HALO), (at >= HALO) & (at < HALO + OWN), (at >= HALO + OWN) & (at < SEGMENT)))
        for f in range(2):
            for t in range(BLOCK):
                own = [g_own[o][f, t] for o in range(rows)]
                first = [g_left[o][f, t // 2] for o in range(rows)]
                second = [g_right[o][f, t // 2] for o in range(rows)]
                left = [jnp.where(even, second[o], first[o]) for o in range(rows)]
                right = [jnp.where(even, first[o], second[o]) for o in range(rows)]
                odd = (t % 2) * HALO
                for s in range(BLOCK):
                    value = jnp.zeros((K, 128), f32)
                    for o in range(rows):
                        shift = bases[o] + 128 * rows - s * OWN
                        low, mid, high = masks[o]
                        value = jnp.where(low, pltpu.roll(left[o], (shift - odd) % 128, 1), value)
                        value = jnp.where(mid, pltpu.roll(own[o], (shift + HALO) % 128, 1), value)
                        value = jnp.where(high, pltpu.roll(right[o], (shift + SEGMENT - HALO - odd) % 128, 1), value)
                    if f == 0:
                        weights[s * BLOCK + t, :, pl.ds(group * 128, 128)] = value
                        store_pieces(s * BLOCK + t, group, value)
                    else:
                        rhs[s * BLOCK + t, :, pl.ds(group * 128, 128)] = value
        cols = pl.ds(group * 128, 128)
        for m in range(1, LEVELS):
            n, fine, coarse = SIDES[m], OFFSETS[m - 1], OFFSETS[m]
            for s in range(n):
                for t in range(n):
                    corner = fine + (2 * s) * (2 * n) + 2 * t
                    value = weights[corner, :, cols] + weights[corner + 1, :, cols]
                    value = value + (weights[corner + 2 * n, :, cols] + weights[corner + 2 * n + 1, :, cols])
                    weights[coarse + s * n + t, :, cols] = value
                    store_pieces(coarse + s * n + t, group, value)
        for slot in range(sum(COUNTS), SLOTS):
            store_pieces(slot, group, jnp.zeros((K, 128), f32))

    flat_inverse = inverse.reshape(groups * SLOTS * ROWS, 128)
    column = lanes_of((8, 128)) % SEGMENT
    inside = ((place[1] > 0) | (column >= HALO)) & ((place[1] < place[2] - 1) | (column < HALO + OWN))
    damped = jnp.where(inside, DAMPING, 0.0).astype(f32)
    half = K // 2
    tables = ((blocks, 0, COUNTS[0]), (coarse_blocks, COUNTS[0], SLOTS - COUNTS[0]))

    for group, (table, offset, count) in ((x, y) for x in range(groups) for y in tables):
        flat_blocks = table.reshape(groups * count * ROWS, 128)

        def multiply(g, group=group, table=table, offset=offset):
            for i in range(4):
                pair = jnp.dot(outer[...], pieces[group, offset // 2 + g * 4 + i], preferred_element_type=f32)
                table[group, g * 8 + 2 * i, pl.ds(0, K * K), :] = pair[:, :128]
                table[group, g * 8 + 2 * i + 1, pl.ds(0, K * K), :] = pair[:, 128:]

        def invert(g, carry, group=group, flat_blocks=flat_blocks, offset=offset, count=count, multiply=multiply):
            slot = offset + g * 8 + lax.broadcasted_iota(jnp.int32, (8, 128), 0)
            scale = jnp.where(
                slot < OFFSETS[1], 4.0, jnp.where(slot < OFFSETS[2], 8.0, jnp.where(slot < OFFSETS[3], 16.0, 32.0))
            ).astype(f32)
            source = (group * count + g * 8) * ROWS
            target = (group * SLOTS + offset + g * 8) * ROWS

            def load(k, l):
                value = flat_blocks[pl.ds(source + l * K + k, 8, stride=ROWS), :]
                return value + scale * prior[k] if k == l else value

            def store(k, l, value):
                value = value * damped
                flat_inverse[pl.ds(target + l * K + k, 8, stride=ROWS), :] = value
                if k != l:
                    flat_inverse[pl.ds(target + k * K + l, 8, stride=ROWS), :] = value

            for i in range(half):
                for j in range(half):
                    work[0, i * half + j] = load(half + j, i)
            for i in range(half):
                for j in range(i + 1):
                    work[2, i * half + j] = load(half + i, half + j)
            first = {(i, j): load(i, j) for i in range(half) for j in range(i + 1)}
            multiply(jnp.minimum(g + 1, count // 8 - 1))
            first = symmetric_inverse(first, half)
            for j in range(half):
                b = [work[0, i * half + j] for i in range(half)]
                for i in range(half):
                    work[1, i * half + j] = sum(first[max(i, h), min(i, h)] * b[h] for h in range(half))
            for i in range(half):
                for j in range(i + 1):
                    work[3, i * half + j] = first[i, j]
            schur = {(i, j): work[2, i * half + j] for i in range(half) for j in range(i + 1)}
            for h in range(half):
                b = [work[0, h * half + j] for j in range(half)]
                y = [work[1, h * half + j] for j in range(half)]
                for i in range(half):
                    for j in range(i + 1):
                        schur[i, j] = schur[i, j] - b[i] * y[j]
            second = symmetric_inverse(schur, half)
            for (i, j), value in second.items():
                store(half + i, half + j, value)
            for i in range(half):
                y = [work[1, i * half + j] for j in range(half)]
                for j in range(half):
                    z = sum(y[h] * second[max(h, j), min(h, j)] for h in range(half))
                    work[0, i * half + j] = z
                    store(half + j, i, -z)
            first = {(i, j): work[3, i * half + j] for i in range(half) for j in range(i + 1)}
            for h in range(half):
                z = [work[0, i * half + h] for i in range(half)]
                y = [work[1, i * half + h] for i in range(half)]
                for i in range(half):
                    for j in range(i + 1):
                        first[i, j] = first[i, j] + z[i] * y[j]
            for (i, j), value in first.items():
                store(i, j, value)
            return carry

        multiply(0)
        lax.fori_loop(0, count // 8, invert, 0)


def beside(read, m, s, t, above, below):
    n = SIDES[m]
    total = read(s - 1, t) if s > 0 else roll(read(n - 1, t), 1)
    total = total + (read(s + 1, t) if s < n - 1 else roll(read(0, t), -1))
    total = total + (read(s, t - 1) if t > 0 else jnp.where(above, roll(read(s, n - 1), SEGMENT), 0.0))
    return total + (read(s, t + 1) if t < n - 1 else jnp.where(below, roll(read(s, 0), -SEGMENT), 0.0))


def block_product(table, first, count, source, finish):
    def one(i, carry):
        for group in range(table.shape[0]):
            cols = pl.ds(group * 128, 128)
            total = None
            for l in range(K):
                term = table[group, first + i, pl.ds(l * K, K), :] * source[i, pl.ds(l, 1), cols]
                total = term if total is None else total + term
            finish(i, cols, total)
        return carry

    lax.fori_loop(0, count, one, 0, unroll=min(count, 16))


def v_cycle(inverse, prior, b, v, d, w):
    width = b[0].shape[-1]
    lane = lanes_of((K, width))
    above, below = lane >= SEGMENT, lane < width - SEGMENT
    weight = [jnp.broadcast_to(prior[...] * 2.0**m, (K, width)) for m in range(LEVELS)]

    def sweep(m, keep=None):
        n = SIDES[m]
        for s in range(n):
            for t in range(n):
                near = beside(lambda x, y: v[m][x * n + y], m, s, t, above, below)
                w[m][s * n + t] = b[m][s * n + t] + weight[m] * near

        def finish(i, cols, total):
            old = v[m][i, :, cols]
            v[m][i, :, cols] = 0.3 * old + total
            if keep is not None:
                keep[i, :, cols] = total - 0.4 * old

        block_product(inverse, OFFSETS[m], COUNTS[m], w[m], finish)

    def begin(m):
        def finish(i, cols, total):
            v[m][i, :, cols] = total

        block_product(inverse, OFFSETS[m], COUNTS[m], b[m], finish)

    for m in range(LEVELS - 1):
        n = SIDES[m]
        begin(m)
        sweep(m, d[m])
        for s in range(0, n, 2):
            for t in range(0, n, 2):
                near, own = None, None
                for x, y in ((s, t), (s, t + 1), (s + 1, t), (s + 1, t + 1)):
                    one = beside(lambda x, y: d[m][x * n + y], m, x, y, above, below)
                    near = one if near is None else near + one
                    one = b[m][x * n + y]
                    own = one if own is None else own + one
                b[m + 1][(s // 2) * (n // 2) + t // 2] = 0.09 * own + weight[m] * near
    begin(LEVELS - 1)
    for _ in range(COARSE_SWEEPS - 1):
        sweep(LEVELS - 1)
    for m in range(LEVELS - 2, -1, -1):
        n = SIDES[m]
        for s in range(n):
            for t in range(n):
                v[m][s * n + t] = v[m][s * n + t] + v[m + 1][(s // 2) * (n // 2) + t // 2]
        sweep(m)
        sweep(m)


def iterate_kernel(step, last, *refs):
    refs = list(refs)
    place, prior, blocks, inverse, residual_in = (refs.pop(0) for _ in range(5))
    if step > 0:
        sums, edge_a, edge_b, z_in, az_in = (refs.pop(0) for _ in range(5))
    if step > 1:
        old, x_in, p_in, ap_in = (refs.pop(0) for _ in range(4))
    if last:
        parts, scalars, packed, residual, x, p, ap, z_out, az_out = (refs.pop(0) for _ in range(9))
    else:
        parts, z_out, az_out, send_a, send_b = (refs.pop(0) for _ in range(5))
        if step > 0:
            scalars, residual, x, p, ap = (refs.pop(0) for _ in range(5))
    b, v, d, w = (refs[i * LEVELS : (i + 1) * LEVELS] for i in range(4))
    width = z_out.shape[-1]
    lane = lanes_of((K, width))
    column = lane % SEGMENT
    mine = (column >= HALO) & (column < HALO + OWN)
    even = place[1] % 2 == 0
    count = COUNTS[0]
    if step > 0:
        gamma, alpha, beta, energy = coefficients(sums, old if step > 1 else None)
        scalars[...] = jnp.concatenate(
            [jnp.broadcast_to(gamma, (1, 128)), jnp.broadcast_to(energy, (1, 128)), jnp.zeros((6, 128), f32)], axis=0
        )
        left_side, right_side = column < HALO, column >= HALO + OWN
        for i in range(count // 4):
            left = jnp.where(even, edge_b[i], edge_a[i])
            right = jnp.where(even, edge_a[i], edge_b[i])
            for g in range(4):
                at = 4 * i + g
                image = jnp.where(left_side, roll(left, -HALO * g), az_in[at])
                image = jnp.where(right_side, roll(right, SEGMENT - HALO - HALO * g), image)
                direction = z_in[at]
                if step > 1:
                    direction = direction + beta * p_in[at]
                    image = image + beta * ap_in[at]
                p[at] = direction
                ap[at] = image
                x[at] = x_in[at] + alpha * direction if step > 1 else alpha * direction
                left_over = residual_in[at] - alpha * image
                residual[at] = left_over
                b[0][at] = left_over
    else:
        for at in range(count):
            b[0][at] = residual_in[at]

    v_cycle(inverse, prior, b, v, d, w)

    above, below = lane >= SEGMENT, lane < width - SEGMENT
    weight = jnp.broadcast_to(prior[...], (K, width))
    n = SIDES[0]
    for s in range(n):
        for t in range(n):
            near = beside(lambda x, y: v[0][x * n + y], 0, s, t, above, below)
            w[0][s * n + t] = weight * (4.0 * v[0][s * n + t] - near)

    def finish(i, cols, total):
        az_out[i, :, cols] = total + w[0][i, :, cols]
        z_out[i, :, cols] = v[0][i, :, cols]

    block_product(blocks, 0, count, v[0], finish)

    names = 3 if step > 0 else 2
    totals = [jnp.zeros((K, width), f32) for _ in range(names)]
    for at in range(count):
        z = z_out[at]
        totals[0] = totals[0] + z * b[0][at]
        totals[1] = totals[1] + z * az_out[at]
        if step > 0:
            totals[2] = totals[2] + z * ap[at]
    rows = []
    for total in totals:
        total = jnp.sum(jnp.where(mine, total, 0.0), axis=0, keepdims=True)
        rows.append(sum(total[:, g * 128 : (g + 1) * 128] for g in range(width // 128)))
    rows.append(jnp.zeros((8 - names, 128), f32))
    tile = jnp.concatenate(rows, axis=0)
    for i in range(parts.shape[0]):
        parts[i] = tile
    if last:
        tile = refs[-1]
        for i, source in enumerate((x, z_out, p)):
            pack(place, source, tile)
            back = lax.dot_general(
                tile[...], lane_order(), (((1,), (1,)), ((), ())), precision=highest, preferred_element_type=f32
            )
            packed[i] = back.reshape(K, BLOCK, 128)
    else:
        for i in range(count // 4):
            left, right = None, None
            for g in range(4):
                value = az_out[4 * i + g]
                low, high = roll(value, HALO * g - HALO), roll(value, HALO * g - OWN)
                here = (column >= HALO * g) & (column < HALO * g + HALO)
                left = low if left is None else jnp.where(here, low, left)
                right = high if right is None else jnp.where(here, high, right)
            send_a[i] = jnp.where(even, right, left)
            send_b[i] = jnp.where(even, left, right)


def coefficients(sums, old):
    total = sums[0]
    for i in range(1, sums.shape[0]):
        total = total + sums[i]
    total = jnp.sum(total, axis=1, keepdims=True)
    gamma, energy = total[0:1], total[1:2]
    beta = None
    if old is not None:
        beta = gamma / old[0:1, 0:1]
        energy = energy + beta * (2.0 * total[2:3] + beta * old[1:2, 0:1])
    return gamma, gamma / energy, beta, energy


def pack(place, source, tile):
    group = pl.ds(pl.multiple_of((place[0] // 4) * 128, 128), 128)
    base = (place[0] % 4) * SEGMENT + HALO
    lane = lanes_of((K, 128))
    for t in range(BLOCK):
        packed = None
        for s in range(BLOCK):
            value = pltpu.roll(source[s * BLOCK + t, :, group], (128 + s * OWN - base) % 128, 1)
            packed = value if packed is None else jnp.where(lane >= s * OWN, value, packed)
        tile[pl.ds(t, K, stride=BLOCK), :] = packed


def finish_kernel(sums, old, packed, out):
    _, alpha, beta, _ = coefficients(sums, old)
    alpha, beta = jnp.broadcast_to(alpha, (BLOCK, 128)), jnp.broadcast_to(beta, (BLOCK, 128))
    for k in range(K):
        out[k] = packed[0, k] + alpha * (packed[1, k] + beta * packed[2, k])


def gather(value):
    rows = lax.axis_size("gx")
    held = {0: value}
    bit = rows // 2
    while bit:
        pairs = [(i, i ^ bit) for i in range(rows)]
        for o in list(held):
            held[o ^ bit] = lax.ppermute(held[o], "gx", pairs)
        bit //= 2
    return [held[o] for o in range(rows)]


def local(beta, design, prior, kept, removed, removed_labels):
    rows, cols = lax.axis_size("gx"), lax.axis_size("gy")
    width = rows * SEGMENT
    place = jnp.stack([lax.axis_index("gx"), lax.axis_index("gy"), jnp.int32(cols)]).astype(jnp.int32)
    pairs = [(i, i ^ 1) for i in range(cols)]
    others = [(0, 0)] + [(i, ((i + 1) ^ 1) - 1) for i in range(1, cols - 1)] + [(cols - 1, cols - 1)]
    others = others[1:-1]

    def shape(*dims, dtype=f32):
        return jax.ShapeDtypeStruct(dims, dtype)

    own, edge_a, edge_b = pl.pallas_call(
        prepare_kernel,
        out_shape=[shape(2, 8, K, 128), shape(2, 4, K, 128), shape(2, 4, K, 128)],
        in_specs=[SMEM, SMEM] + [VMEM] * 4,
        out_specs=[VMEM] * 3,
        scratch_shapes=[pltpu.VMEM((2 * K * BLOCK, 128), f32)],
        name="prepare",
    )(place, design, beta, kept, removed, removed_labels)
    edge_a = lax.ppermute(edge_a, "gy", pairs)
    edge_b = lax.ppermute(edge_b, "gy", others)
    gathered = gather(own) + gather(edge_a) + gather(edge_b)

    products = (design[:, :, None] * design[:, None, :]).reshape(K, K * K).T
    parts, rest = [], products
    for _ in range(3):
        part = lax.reduce_precision(rest, 8, 7)
        parts.append(part)
        rest = rest - part
    outer = jnp.concatenate([parts[a] for a, _ in SPLITS], axis=1).astype(jnp.bfloat16)
    prior_rows = prior[:, None]

    field = shape(COUNTS[0], K, width)
    blocks, inverse, residual = pl.pallas_call(
        setup_kernel,
        out_shape=[shape(width // 128, n, ROWS, 128) for n in (COUNTS[0], SLOTS)] + [field],
        in_specs=[SMEM, SMEM] + [VMEM] * (1 + len(gathered)),
        out_specs=[VMEM] * 3,
        scratch_shapes=[
            pltpu.VMEM((SLOTS, K, width), f32),
            pltpu.VMEM((width // 128, SLOTS // 2, len(SPLITS) * K, 256), jnp.bfloat16),
            pltpu.VMEM((width // 128, SLOTS - COUNTS[0], ROWS, 128), f32),
            pltpu.VMEM((4, K * K // 4, 8, 128), f32),
        ],
        compiler_params=params(24 if width == 128 else 60),
        name="setup",
    )(place, prior, outer, *gathered)

    levels = [pltpu.VMEM((n, K, width), f32) for n in COUNTS] * 4
    whole = pltpu.VMEM((COUNTS[0], K, width), f32)
    edge = shape(COUNTS[0] // 4, K, width)
    parts = shape(cols, 8, 128)
    state = ()
    for step in range(ITERS):
        last = step == ITERS - 1
        operands = (place, prior_rows, blocks, inverse, residual) + state
        if last:
            shapes = [parts, shape(8, 128), shape(3, *beta.shape)]
            scratch = [whole] * 6 + levels + [pltpu.VMEM((K * BLOCK, 128), f32)]
        else:
            shapes = [parts, field, field, edge, edge]
            if step > 0:
                shapes += [shape(8, 128), field, field, field, field]
            scratch = levels
        outs = pl.pallas_call(
            functools.partial(iterate_kernel, step, last),
            out_shape=shapes,
            in_specs=[SMEM] + [VMEM] * (len(operands) - 1),
            out_specs=[VMEM] * len(shapes),
            scratch_shapes=scratch,
            compiler_params=params(24 if width == 128 else 60),
            name=f"iterate_{step}",
        )(*operands)
        sums = lax.all_to_all(outs[0], "gy", 0, 0, tiled=True)
        if not last:
            edge_a = lax.ppermute(outs[3], "gy", pairs)
            edge_b = lax.ppermute(outs[4], "gy", others)
            state = (sums, edge_a, edge_b, outs[1], outs[2])
            if step > 0:
                residual = outs[6]
                state += (outs[5], outs[7], outs[8], outs[9])
    return pl.pallas_call(
        finish_kernel,
        out_shape=shape(*beta.shape),
        in_specs=[VMEM] * 3,
        out_specs=VMEM,
        name="finish",
    )(sums, outs[1], outs[2])


def solution(mesh):
    placed = (
        P(None, "gx", "gy"),
        P(),
        P(),
        P(None, "gx", "gy"),
        P(None, "gx", "gy"),
        P(None, "gx", "gy"),
    )
    return jax.shard_map(
        local, mesh=mesh, in_specs=placed, out_specs=P(None, "gx", "gy"), check_vma=False
    )
```

```python
import functools

import jax
import jax.numpy as jnp
from jax import lax
from jax.experimental import pallas as pl
from jax.experimental.pallas import tpu as pltpu
from jax.sharding import PartitionSpec as P

LEVELS = 4
COARSE_SWEEPS = 4
K = 16
BLOCK = 8
SEGMENT = 32
HALO = 8
OWN = 16
DAMPING = 0.7

highest = lax.Precision.HIGHEST
f32 = jnp.float32

SIDES = [BLOCK >> m for m in range(LEVELS)]
COUNTS = [n * n for n in SIDES]
OFFSETS = [sum(COUNTS[:m]) for m in range(LEVELS)]
SLOTS = -(-sum(COUNTS) // 8) * 8
ROWS = K * K + 8
SPLITS = ((0, 0), (0, 1), (0, 2), (1, 0), (1, 1), (2, 0))

VMEM = pl.BlockSpec(memory_space=pltpu.VMEM)
SMEM = pl.BlockSpec(memory_space=pltpu.SMEM)


def params(mib):
    return pltpu.CompilerParams(vmem_limit_bytes=mib << 20)


def lanes_of(shape):
    return lax.broadcasted_iota(jnp.int32, shape, len(shape) - 1)


def roll(x, shift):
    shift = shift % x.shape[-1]
    return x if shift == 0 else pltpu.roll(x, shift, x.ndim - 1)


def lane_order():
    row = lax.broadcasted_iota(jnp.int32, (128, 128), 0)
    lane = lax.broadcasted_iota(jnp.int32, (128, 128), 1)
    return (lane == (row % BLOCK) * OWN + row // BLOCK).astype(f32)


def prepare_kernel(place, design, beta, kept, removed, labels, own, edge_a, edge_b, tile):
    probs = []
    for j in range(K):
        logit = sum(design[j, k] * beta[k] for k in range(K))
        prob = 1.0 / (1.0 + jnp.exp(-logit))
        probs.append(removed[j].astype(f32) * prob - labels[j].astype(f32))
        tile[pl.ds(j * BLOCK, BLOCK), :] = kept[j].astype(f32) * prob * (1.0 - prob)
    for k in range(K):
        tile[pl.ds((K + k) * BLOCK, BLOCK), :] = sum(design[j, k] * probs[j] for j in range(K))
    tile[...] = jnp.dot(tile[...], lane_order(), precision=highest, preferred_element_type=f32)
    even = place[1] % 2 == 0
    low = lanes_of((K, 128)) % OWN < HALO
    for f in range(2):
        rows = [tile[pl.ds(f * K * BLOCK + t, K, stride=BLOCK), :] for t in range(BLOCK)]
        for t in range(BLOCK):
            own[f, t] = rows[t]
        for i in range(BLOCK // 2):
            left = jnp.where(low, rows[2 * i], roll(rows[2 * i + 1], HALO))
            right = jnp.where(low, roll(rows[2 * i], -HALO), rows[2 * i + 1])
            edge_a[f, i] = jnp.where(even, right, left)
            edge_b[f, i] = jnp.where(even, left, right)


def symmetric_inverse(a, n):
    a = dict(a)
    for p in range(n):
        d = 1.0 / a[p, p]
        col = {i: a[max(i, p), min(i, p)] for i in range(n) if i != p}
        fac = {i: col[i] * d for i in col}
        for i in col:
            for j in col:
                if j <= i:
                    a[i, j] = a[i, j] - fac[i] * col[j]
        for i in col:
            a[max(i, p), min(i, p)] = fac[i]
        a[p, p] = -d
    return {ij: -x for ij, x in a.items()}


def setup_kernel(place, prior, outer, *refs):
    rows = (len(refs) - 8) // 3
    g_own, g_left, g_right = (refs[i * rows : (i + 1) * rows] for i in range(3))
    blocks, inverse, rhs, prior_rows, weights, pieces, coarse_blocks, work = refs[3 * rows :]
    width = rhs.shape[-1]
    groups = width // 128
    lane = lanes_of((K, 128))
    even = place[1] % 2 == 0
    channel = lax.broadcasted_iota(jnp.int32, (K, width), 0)
    prior_rows[...] = sum(jnp.where(channel == k, prior[k], 0.0) for k in range(K))

    def store_pieces(slot, group, rest):
        cols = pl.ds((slot % 2) * 128, 128)
        parts = []
        for _ in range(3):
            part = rest.astype(jnp.bfloat16)
            parts.append(part)
            rest = rest - part.astype(f32)
        for i, (_, b) in enumerate(SPLITS):
            pieces[group, slot // 2, pl.ds(i * K, K), cols] = parts[b]

    for group in range(groups):
        bases = [(place[0] ^ o) * SEGMENT - group * 128 for o in range(rows)]
        masks = []
        for base in bases:
            at = lane - base
            masks.append(((at >= 0) & (at < HALO), (at >= HALO) & (at < HALO + OWN), (at >= HALO + OWN) & (at < SEGMENT)))
        for f in range(2):
            for t in range(BLOCK):
                own = [g_own[o][f, t] for o in range(rows)]
                first = [g_left[o][f, t // 2] for o in range(rows)]
                second = [g_right[o][f, t // 2] for o in range(rows)]
                left = [jnp.where(even, second[o], first[o]) for o in range(rows)]
                right = [jnp.where(even, first[o], second[o]) for o in range(rows)]
                odd = (t % 2) * HALO
                for s in range(BLOCK):
                    value = jnp.zeros((K, 128), f32)
                    for o in range(rows):
                        shift = bases[o] + 128 * rows - s * OWN
                        low, mid, high = masks[o]
                        value = jnp.where(low, pltpu.roll(left[o], (shift - odd) % 128, 1), value)
                        value = jnp.where(mid, pltpu.roll(own[o], (shift + HALO) % 128, 1), value)
                        value = jnp.where(high, pltpu.roll(right[o], (shift + SEGMENT - HALO - odd) % 128, 1), value)
                    if f == 0:
                        weights[s * BLOCK + t, :, pl.ds(group * 128, 128)] = value
                        store_pieces(s * BLOCK + t, group, value)
                    else:
                        rhs[s * BLOCK + t, :, pl.ds(group * 128, 128)] = value
        cols = pl.ds(group * 128, 128)
        for m in range(1, LEVELS):
            n, fine, coarse = SIDES[m], OFFSETS[m - 1], OFFSETS[m]
            for s in range(n):
                for t in range(n):
                    corner = fine + (2 * s) * (2 * n) + 2 * t
                    value = weights[corner, :, cols] + weights[corner + 1, :, cols]
                    value = value + (weights[corner + 2 * n, :, cols] + weights[corner + 2 * n + 1, :, cols])
                    weights[coarse + s * n + t, :, cols] = value
                    store_pieces(coarse + s * n + t, group, value)
        for slot in range(sum(COUNTS), SLOTS):
            store_pieces(slot, group, jnp.zeros((K, 128), f32))

    flat_inverse = inverse.reshape(groups * SLOTS * ROWS, 128)
    column = lanes_of((8, 128)) % SEGMENT
    inside = ((place[1] > 0) | (column >= HALO)) & ((place[1] < place[2] - 1) | (column < HALO + OWN))
    damped = jnp.where(inside, DAMPING, 0.0).astype(f32)
    half = K // 2
    tables = ((blocks, 0, COUNTS[0]), (coarse_blocks, COUNTS[0], SLOTS - COUNTS[0]))

    for group, (table, offset, count) in ((x, y) for x in range(groups) for y in tables):
        flat_blocks = table.reshape(groups * count * ROWS, 128)

        def multiply(g, group=group, table=table, offset=offset):
            for i in range(4):
                pair = jnp.dot(outer[...], pieces[group, offset // 2 + g * 4 + i], preferred_element_type=f32)
                table[group, g * 8 + 2 * i, pl.ds(0, K * K), :] = pair[:, :128]
                table[group, g * 8 + 2 * i + 1, pl.ds(0, K * K), :] = pair[:, 128:]

        def invert(g, carry, group=group, flat_blocks=flat_blocks, offset=offset, count=count, multiply=multiply):
            slot = offset + g * 8 + lax.broadcasted_iota(jnp.int32, (8, 128), 0)
            scale = jnp.where(
                slot < OFFSETS[1], 4.0, jnp.where(slot < OFFSETS[2], 8.0, jnp.where(slot < OFFSETS[3], 16.0, 32.0))
            ).astype(f32)
            source = (group * count + g * 8) * ROWS
            target = (group * SLOTS + offset + g * 8) * ROWS

            def load(k, l):
                value = flat_blocks[pl.ds(source + l * K + k, 8, stride=ROWS), :]
                return value + scale * prior[k] if k == l else value

            def store(k, l, value):
                value = value * damped
                flat_inverse[pl.ds(target + l * K + k, 8, stride=ROWS), :] = value
                if k != l:
                    flat_inverse[pl.ds(target + k * K + l, 8, stride=ROWS), :] = value

            for i in range(half):
                for j in range(half):
                    work[0, i * half + j] = load(half + j, i)
            for i in range(half):
                for j in range(i + 1):
                    work[2, i * half + j] = load(half + i, half + j)
            first = {(i, j): load(i, j) for i in range(half) for j in range(i + 1)}
            multiply(jnp.minimum(g + 1, count // 8 - 1))
            first = symmetric_inverse(first, half)
            for j in range(half):
                b = [work[0, i * half + j] for i in range(half)]
                for i in range(half):
                    work[1, i * half + j] = sum(first[max(i, h), min(i, h)] * b[h] for h in range(half))
            for i in range(half):
                for j in range(i + 1):
                    work[3, i * half + j] = first[i, j]
            schur = {(i, j): work[2, i * half + j] for i in range(half) for j in range(i + 1)}
            for h in range(half):
                b = [work[0, h * half + j] for j in range(half)]
                y = [work[1, h * half + j] for j in range(half)]
                for i in range(half):
                    for j in range(i + 1):
                        schur[i, j] = schur[i, j] - b[i] * y[j]
            second = symmetric_inverse(schur, half)
            for (i, j), value in second.items():
                store(half + i, half + j, value)
            for i in range(half):
                y = [work[1, i * half + j] for j in range(half)]
                for j in range(half):
                    z = sum(y[h] * second[max(h, j), min(h, j)] for h in range(half))
                    work[0, i * half + j] = z
                    store(half + j, i, -z)
            first = {(i, j): work[3, i * half + j] for i in range(half) for j in range(i + 1)}
            for h in range(half):
                z = [work[0, i * half + h] for i in range(half)]
                y = [work[1, i * half + h] for i in range(half)]
                for i in range(half):
                    for j in range(i + 1):
                        first[i, j] = first[i, j] + z[i] * y[j]
            for (i, j), value in first.items():
                store(i, j, value)
            return carry

        multiply(0)
        lax.fori_loop(0, count // 8, invert, 0)


def beside(read, m, s, t, above, below):
    n = SIDES[m]
    total = read(s - 1, t) if s > 0 else roll(read(n - 1, t), 1)
    total = total + (read(s + 1, t) if s < n - 1 else roll(read(0, t), -1))
    total = total + (read(s, t - 1) if t > 0 else jnp.where(above, roll(read(s, n - 1), SEGMENT), 0.0))
    return total + (read(s, t + 1) if t < n - 1 else jnp.where(below, roll(read(s, 0), -SEGMENT), 0.0))


def block_product(table, first, count, source, finish):
    def one(i, carry):
        for group in range(table.shape[0]):
            cols = pl.ds(group * 128, 128)
            total = None
            for l in range(K):
                term = table[group, first + i, pl.ds(l * K, K), :] * source[i, pl.ds(l, 1), cols]
                total = term if total is None else total + term
            finish(i, cols, total)
        return carry

    lax.fori_loop(0, count, one, 0, unroll=min(count, 16))


def v_cycle(inverse, prior, b, v, d, w):
    width = b[0].shape[-1]
    lane = lanes_of((K, width))
    above, below = lane >= SEGMENT, lane < width - SEGMENT
    weight = [prior[...] * 2.0**m for m in range(LEVELS)]

    def sweep(m, keep=None):
        n = SIDES[m]
        for s in range(n):
            for t in range(n):
                near = beside(lambda x, y: v[m][x * n + y], m, s, t, above, below)
                w[m][s * n + t] = b[m][s * n + t] + weight[m] * near

        def finish(i, cols, total):
            old = v[m][i, :, cols]
            v[m][i, :, cols] = 0.3 * old + total
            if keep is not None:
                keep[i, :, cols] = total - 0.4 * old

        block_product(inverse, OFFSETS[m], COUNTS[m], w[m], finish)

    def begin(m):
        def finish(i, cols, total):
            v[m][i, :, cols] = total

        block_product(inverse, OFFSETS[m], COUNTS[m], b[m], finish)

    for m in range(LEVELS - 1):
        n = SIDES[m]
        begin(m)
        sweep(m, d[m])
        for s in range(0, n, 2):
            for t in range(0, n, 2):
                near, own = None, None
                for x, y in ((s, t), (s, t + 1), (s + 1, t), (s + 1, t + 1)):
                    one = beside(lambda x, y: d[m][x * n + y], m, x, y, above, below)
                    near = one if near is None else near + one
                    one = b[m][x * n + y]
                    own = one if own is None else own + one
                b[m + 1][(s // 2) * (n // 2) + t // 2] = 0.09 * own + weight[m] * near
    begin(LEVELS - 1)
    for _ in range(COARSE_SWEEPS - 1):
        sweep(LEVELS - 1)
    for m in range(LEVELS - 2, -1, -1):
        n = SIDES[m]
        for s in range(n):
            for t in range(n):
                v[m][s * n + t] = v[m][s * n + t] + v[m + 1][(s // 2) * (n // 2) + t // 2]
        sweep(m)
        sweep(m)


def dots(rows, width, mine):
    totals = [jnp.zeros((K, width), f32) for _ in rows]
    for at in range(COUNTS[0]):
        for i, (one, other) in enumerate(rows):
            totals[i] = totals[i] + one[at] * other[at]
    lines = []
    for total in totals:
        total = jnp.sum(jnp.where(mine, total, 0.0), axis=0, keepdims=True)
        lines.append(sum(total[:, g * 128 : (g + 1) * 128] for g in range(width // 128)))
    if len(rows) % 8:
        lines.append(jnp.zeros((-len(rows) % 8, 128), f32))
    return jnp.concatenate(lines, axis=0)


def summed(sums):
    total = sums[0]
    for i in range(1, sums.shape[0]):
        total = total + sums[i]
    total = jnp.sum(total, axis=1, keepdims=True)
    return [total[i : i + 1] for i in range(total.shape[0])]


def kept_apart(energy, whole):
    return jnp.maximum(energy, 1e-7 * whole)


def first_pair(sums):
    g0, g1, e00, e01, e11 = summed(sums)[:5]
    ratio = e01 / e00
    energy = kept_apart(e11 - ratio * e01, e11)
    return e00, energy, ratio, g0 / e00, (g1 - ratio * g0) / energy


def second_pair(sums, e0, e1):
    h0, h1, h2, h3, a20, a21, a22, a30, a31, a32, a33 = summed(sums)[:11]
    l20, l21, l30, l31 = a20 / e0, a21 / e1, a30 / e0, a31 / e1
    e2 = kept_apart(a22 - l20 * a20 - l21 * a21, a22)
    cross = a32 - l20 * a30 - l21 * a31
    l32 = cross / e2
    e3 = kept_apart(a33 - l30 * a30 - l31 * a31 - l32 * cross, a33)
    n2 = h2 - l20 * h0 - l21 * h1
    n3 = h3 - l30 * h0 - l31 * h1 - l32 * n2
    c3 = n3 / e3
    c2 = n2 / e2 - l32 * c3
    return h0 / e0 - l20 * c2 - l30 * c3, h1 / e1 - l21 * c2 - l31 * c3, c2, c3


def iterate_kernel(step, *refs):
    refs = list(refs)
    take = lambda n: [refs.pop(0) for _ in range(n)]
    place, prior, blocks, inverse, rhs = take(5)
    if step == 0:
        z0, az0, send_a, send_b = take(4)
        z, az = z0, az0
    elif step == 1:
        edge_a, edge_b, z0, az0, parts, full, w1, aw1, send_a, send_b = take(10)
        z, az = w1, aw1
    elif step == 2:
        sums, edge_a, edge_b, z0, az0, w1, aw1 = take(7)
        scalars, p1, ap1, left_over, z2, az2, send_a, send_b = take(8)
        z, az = z2, az2
    else:
        edge_a, edge_b, z0, az0, p1, ap1, z2, az2 = take(8)
        parts, packed, w3, aw3 = take(4)
        z, az = w3, aw3
    b, v, d, w = (take(LEVELS) for _ in range(4))
    width = z.shape[-1]
    lane = lanes_of((K, width))
    column = lane % SEGMENT
    mine = (column >= HALO) & (column < HALO + OWN)
    even = place[1] % 2 == 0
    count = COUNTS[0]

    def arrived(own):
        left_side, right_side = column < HALO, column >= HALO + OWN
        for i in range(count // 4):
            left = jnp.where(even, edge_b[i], edge_a[i])
            right = jnp.where(even, edge_a[i], edge_b[i])
            for g in range(4):
                at = 4 * i + g
                value = jnp.where(left_side, roll(left, -HALO * g), own[at])
                yield at, jnp.where(right_side, roll(right, SEGMENT - HALO - HALO * g), value)

    if step == 0:
        for at in range(count):
            b[0][at] = rhs[at]
    elif step == 1:
        for at, image in arrived(az0):
            full[at] = image
            b[0][at] = rhs[at] - image
    elif step == 2:
        e0, e1, ratio, c0, c1 = first_pair(sums)
        rows = [jnp.broadcast_to(x, (1, 128)) for x in (e0, e1, c0, c1)]
        scalars[...] = jnp.concatenate(rows + [jnp.zeros((4, 128), f32)], axis=0)
        for at, image in arrived(aw1):
            first = az0[at]
            image = image - ratio * first
            ap1[at] = image
            p1[at] = w1[at] - ratio * z0[at]
            value = rhs[at] - c0 * first - c1 * image
            left_over[at] = value
            b[0][at] = value
    else:
        for at, image in arrived(az2):
            b[0][at] = rhs[at] - image

    v_cycle(inverse, prior, b, v, d, w)

    above, below = lane >= SEGMENT, lane < width - SEGMENT
    weight = prior[...]
    n = SIDES[0]
    for s in range(n):
        for t in range(n):
            near = beside(lambda x, y: v[0][x * n + y], 0, s, t, above, below)
            w[0][s * n + t] = weight * (4.0 * v[0][s * n + t] - near)

    def finish(i, cols, total):
        az[i, :, cols] = total + w[0][i, :, cols]
        z[i, :, cols] = v[0][i, :, cols]

    block_product(blocks, 0, count, v[0], finish)

    if step == 1:
        tile = dots([(z0, rhs), (w1, rhs), (z0, az0), (w1, az0), (w1, aw1)], width, mine)
    elif step == 3:
        pairs = [(z0, rhs), (p1, rhs), (z2, rhs), (w3, rhs)]
        pairs += [(z2, az0), (z2, ap1), (z2, az2), (w3, az0), (w3, ap1), (w3, az2), (w3, aw3)]
        tile = dots(pairs, width, mine)
    if step % 2:
        for i in range(parts.shape[0]):
            parts[i] = tile
    if step == 3:
        tile = refs[-1]
        for i, source in enumerate((z0, p1, z2, w3)):
            pack(place, source, tile)
            back = lax.dot_general(
                tile[...], lane_order(), (((1,), (1,)), ((), ())), precision=highest, preferred_element_type=f32
            )
            packed[i] = back.reshape(K, BLOCK, 128)
    else:
        for i in range(count // 4):
            left, right = None, None
            for g in range(4):
                value = az[4 * i + g]
                low, high = roll(value, HALO * g - HALO), roll(value, HALO * g - OWN)
                here = (column >= HALO * g) & (column < HALO * g + HALO)
                left = low if left is None else jnp.where(here, low, left)
                right = high if right is None else jnp.where(here, high, right)
            send_a[i] = jnp.where(even, right, left)
            send_b[i] = jnp.where(even, left, right)


def pack(place, source, tile):
    group = pl.ds(pl.multiple_of((place[0] // 4) * 128, 128), 128)
    base = (place[0] % 4) * SEGMENT + HALO
    lane = lanes_of((K, 128))
    for t in range(BLOCK):
        packed = None
        for s in range(BLOCK):
            value = pltpu.roll(source[s * BLOCK + t, :, group], (128 + s * OWN - base) % 128, 1)
            packed = value if packed is None else jnp.where(lane >= s * OWN, value, packed)
        tile[pl.ds(t, K, stride=BLOCK), :] = packed


def finish_kernel(sums, scalars, packed, out):
    e0, e1, c0, c1 = (scalars[i : i + 1, 0:1] for i in range(4))
    d0, d1, d2, d3 = second_pair(sums, e0, e1)
    factors = [jnp.broadcast_to(x, (BLOCK, 128)) for x in (c0 + d0, c1 + d1, d2, d3)]
    for k in range(K):
        out[k] = sum(factors[i] * packed[i, k] for i in range(4))


def gather(value):
    rows = lax.axis_size("gx")
    held = {0: value}
    bit = rows // 2
    while bit:
        pairs = [(i, i ^ bit) for i in range(rows)]
        for o in list(held):
            held[o ^ bit] = lax.ppermute(held[o], "gx", pairs)
        bit //= 2
    return [held[o] for o in range(rows)]


def local(beta, design, prior, kept, removed, removed_labels):
    rows, cols = lax.axis_size("gx"), lax.axis_size("gy")
    width = rows * SEGMENT
    place = jnp.stack([lax.axis_index("gx"), lax.axis_index("gy"), jnp.int32(cols)]).astype(jnp.int32)
    pairs = [(i, i ^ 1) for i in range(cols)]
    others = [(0, 0)] + [(i, ((i + 1) ^ 1) - 1) for i in range(1, cols - 1)] + [(cols - 1, cols - 1)]
    others = others[1:-1]

    def shape(*dims, dtype=f32):
        return jax.ShapeDtypeStruct(dims, dtype)

    own, edge_a, edge_b = pl.pallas_call(
        prepare_kernel,
        out_shape=[shape(2, 8, K, 128), shape(2, 4, K, 128), shape(2, 4, K, 128)],
        in_specs=[SMEM, SMEM] + [VMEM] * 4,
        out_specs=[VMEM] * 3,
        scratch_shapes=[pltpu.VMEM((2 * K * BLOCK, 128), f32)],
        name="prepare",
    )(place, design, beta, kept, removed, removed_labels)
    edge_a = lax.ppermute(edge_a, "gy", pairs)
    edge_b = lax.ppermute(edge_b, "gy", others)
    gathered = gather(own) + gather(edge_a) + gather(edge_b)

    products = (design[:, :, None] * design[:, None, :]).reshape(K, K * K).T
    parts, rest = [], products
    for _ in range(3):
        part = lax.reduce_precision(rest, 8, 7)
        parts.append(part)
        rest = rest - part
    outer = jnp.concatenate([parts[a] for a, _ in SPLITS], axis=1).astype(jnp.bfloat16)

    field = shape(COUNTS[0], K, width)
    blocks, inverse, rhs, prior_rows = pl.pallas_call(
        setup_kernel,
        out_shape=[shape(width // 128, n, ROWS, 128) for n in (COUNTS[0], SLOTS)] + [field, shape(K, width)],
        in_specs=[SMEM, SMEM] + [VMEM] * (1 + len(gathered)),
        out_specs=[VMEM] * 4,
        scratch_shapes=[
            pltpu.VMEM((SLOTS, K, width), f32),
            pltpu.VMEM((width // 128, SLOTS // 2, len(SPLITS) * K, 256), jnp.bfloat16),
            pltpu.VMEM((width // 128, SLOTS - COUNTS[0], ROWS, 128), f32),
            pltpu.VMEM((4, K * K // 4, 8, 128), f32),
        ],
        compiler_params=params(24 if width == 128 else 60),
        name="setup",
    )(place, prior, outer, *gathered)

    levels = [pltpu.VMEM((n, K, width), f32) for n in COUNTS] * 4
    whole = pltpu.VMEM((COUNTS[0], K, width), f32)
    edge = shape(COUNTS[0] // 4, K, width)

    def iterate(step, *operands, shapes, scratch=()):
        return pl.pallas_call(
            functools.partial(iterate_kernel, step),
            out_shape=shapes,
            in_specs=[SMEM] + [VMEM] * (len(operands) + 3),
            out_specs=[VMEM] * len(shapes),
            scratch_shapes=list(scratch[:2]) + levels + list(scratch[2:]),
            compiler_params=params(24 if width == 128 else 60),
            name=f"iterate_{step}",
        )(place, prior_rows, blocks, inverse, *operands)

    def exchange(edge_a, edge_b):
        return lax.ppermute(edge_a, "gy", pairs), lax.ppermute(edge_b, "gy", others)

    def total(parts):
        return lax.all_to_all(parts, "gy", 0, 0, tiled=True)

    z0, az0, *edges = iterate(0, rhs, shapes=[field, field, edge, edge])
    edges = exchange(*edges)
    parts, az0, w1, aw1, *edges = iterate(
        1, rhs, *edges, z0, az0, shapes=[shape(cols, 8, 128), field, field, field, edge, edge]
    )
    sums, edges = total(parts), exchange(*edges)
    scalars, p1, ap1, residual, z2, az2, *edges = iterate(
        2, rhs, sums, *edges, z0, az0, w1, aw1, shapes=[shape(8, 128)] + [field] * 5 + [edge, edge]
    )
    edges = exchange(*edges)
    parts, packed = iterate(
        3,
        residual,
        *edges,
        z0,
        az0,
        p1,
        ap1,
        z2,
        az2,
        shapes=[shape(cols, 16, 128), shape(4, *beta.shape)],
        scratch=[whole, whole, pltpu.VMEM((K * BLOCK, 128), f32)],
    )
    return pl.pallas_call(
        finish_kernel,
        out_shape=shape(*beta.shape),
        in_specs=[VMEM] * 3,
        out_specs=VMEM,
        name="finish",
    )(total(parts), scalars, packed)


def solution(mesh):
    placed = (
        P(None, "gx", "gy"),
        P(),
        P(),
        P(None, "gx", "gy"),
        P(None, "gx", "gy"),
        P(None, "gx", "gy"),
    )
    return jax.shard_map(
        local, mesh=mesh, in_specs=placed, out_specs=P(None, "gx", "gy"), check_vma=False
    )
```

```python
import functools

import jax
import jax.numpy as jnp
from jax import lax
from jax.experimental import pallas as pl
from jax.experimental.pallas import tpu as pltpu
from jax.sharding import PartitionSpec as P

ITERS = 4
LEVELS = 4
COARSE_SWEEPS = 4
K = 16
BLOCK = 8
SEGMENT = 32
HALO = 8
OWN = 16
DAMPING = 0.7

highest = lax.Precision.HIGHEST
f32 = jnp.float32

SIDES = [BLOCK >> m for m in range(LEVELS)]
COUNTS = [n * n for n in SIDES]
OFFSETS = [sum(COUNTS[:m]) for m in range(LEVELS)]
SLOTS = -(-sum(COUNTS) // 8) * 8
ROWS = K * K + 8
GRAM = [(3, 0), (3, 1), (3, 2), (3, 3)] + [(i, -1) for i in range(ITERS)] + [(i, j) for i in range(3) for j in range(i + 1)]
SPLITS = ((0, 0), (0, 1), (0, 2), (1, 0), (1, 1), (2, 0))

VMEM = pl.BlockSpec(memory_space=pltpu.VMEM)
SMEM = pl.BlockSpec(memory_space=pltpu.SMEM)


def params(mib):
    return pltpu.CompilerParams(vmem_limit_bytes=mib << 20)


def lanes_of(shape):
    return lax.broadcasted_iota(jnp.int32, shape, len(shape) - 1)


def roll(x, shift):
    shift = shift % x.shape[-1]
    return x if shift == 0 else pltpu.roll(x, shift, x.ndim - 1)


def lane_order():
    row = lax.broadcasted_iota(jnp.int32, (128, 128), 0)
    lane = lax.broadcasted_iota(jnp.int32, (128, 128), 1)
    return (lane == (row % BLOCK) * OWN + row // BLOCK).astype(f32)


def prepare_kernel(design, prior, beta, kept, removed, labels, own, held, edge_a, edge_b, prior_rows, tile):
    probs = []
    for j in range(K):
        logit = sum(design[j, k] * beta[k] for k in range(K))
        prob = 1.0 / (1.0 + jnp.exp(-logit))
        probs.append(removed[j].astype(f32) * prob - labels[j].astype(f32))
        tile[pl.ds(j * BLOCK, BLOCK), :] = kept[j].astype(f32) * prob * (1.0 - prob)
    for k in range(K):
        tile[pl.ds((K + k) * BLOCK, BLOCK), :] = sum(design[j, k] * probs[j] for j in range(K))
    tile[...] = jnp.dot(tile[...], lane_order(), precision=highest, preferred_element_type=f32)
    channel = lax.broadcasted_iota(jnp.int32, prior_rows.shape, 0)
    prior_rows[...] = sum(jnp.where(channel == k, prior[k], 0.0) for k in range(K))
    even = lax.axis_index("gy") % 2 == 0
    low = lanes_of((K, 128)) % OWN < HALO
    for f in range(2):
        rows = [tile[pl.ds(f * K * BLOCK + t, K, stride=BLOCK), :] for t in range(BLOCK)]
        for t in range(BLOCK):
            own[f, t] = rows[t]
            held[f, t] = rows[t]
        for i in range(BLOCK // 2):
            left = jnp.where(low, rows[2 * i], roll(rows[2 * i + 1], HALO))
            right = jnp.where(low, roll(rows[2 * i], -HALO), rows[2 * i + 1])
            edge_a[f, i] = jnp.where(even, right, left)
            edge_b[f, i] = jnp.where(even, left, right)


def symmetric_inverse(a, n):
    a = dict(a)
    for p in range(n):
        d = 1.0 / a[p, p]
        col = {i: a[max(i, p), min(i, p)] for i in range(n) if i != p}
        fac = {i: col[i] * d for i in col}
        for i in col:
            for j in col:
                if j <= i:
                    a[i, j] = a[i, j] - fac[i] * col[j]
        for i in col:
            a[max(i, p), min(i, p)] = fac[i]
        a[p, p] = -d
    return {ij: -x for ij, x in a.items()}


def setup_kernel(outer, prior_rows, *refs):
    rows = (len(refs) - 7) // 3
    g_own, g_left, g_right = (refs[i * rows : (i + 1) * rows] for i in range(3))
    blocks, inverse, rhs, weights, pieces, coarse_blocks, work = refs[3 * rows :]
    gx, gy = lax.axis_index("gx"), lax.axis_index("gy")
    width = rhs.shape[-1]
    groups = width // 128
    lane = lanes_of((K, 128))
    even = gy % 2 == 0

    def store_pieces(slot, group, rest):
        cols = pl.ds((slot % 2) * 128, 128)
        parts = []
        for _ in range(3):
            part = rest.astype(jnp.bfloat16)
            parts.append(part)
            rest = rest - part.astype(f32)
        for i, (_, b) in enumerate(SPLITS):
            pieces[group, slot // 2, pl.ds(i * K, K), cols] = parts[b]

    for group in range(groups):
        bases = [(gx ^ o) * SEGMENT - group * 128 for o in range(rows)]
        masks = []
        for base in bases:
            at = lane - base
            masks.append(((at >= 0) & (at < HALO), (at >= HALO) & (at < HALO + OWN), (at >= HALO + OWN) & (at < SEGMENT)))
        for f in range(2):
            for t in range(BLOCK):
                own = [g_own[o][f, t] for o in range(rows)]
                first = [g_left[o][f, t // 2] for o in range(rows)]
                second = [g_right[o][f, t // 2] for o in range(rows)]
                left = [jnp.where(even, second[o], first[o]) for o in range(rows)]
                right = [jnp.where(even, first[o], second[o]) for o in range(rows)]
                odd = (t % 2) * HALO
                for s in range(BLOCK):
                    value = jnp.zeros((K, 128), f32)
                    for o in range(rows):
                        shift = bases[o] + 128 * rows - s * OWN
                        low, mid, high = masks[o]
                        value = jnp.where(low, pltpu.roll(left[o], (shift - odd) % 128, 1), value)
                        value = jnp.where(mid, pltpu.roll(own[o], (shift + HALO) % 128, 1), value)
                        value = jnp.where(high, pltpu.roll(right[o], (shift + SEGMENT - HALO - odd) % 128, 1), value)
                    if f == 0:
                        weights[s * BLOCK + t, :, pl.ds(group * 128, 128)] = value
                        store_pieces(s * BLOCK + t, group, value)
                    else:
                        rhs[s * BLOCK + t, :, pl.ds(group * 128, 128)] = value
        cols = pl.ds(group * 128, 128)
        for m in range(1, LEVELS):
            n, fine, coarse = SIDES[m], OFFSETS[m - 1], OFFSETS[m]
            for s in range(n):
                for t in range(n):
                    corner = fine + (2 * s) * (2 * n) + 2 * t
                    value = weights[corner, :, cols] + weights[corner + 1, :, cols]
                    value = value + (weights[corner + 2 * n, :, cols] + weights[corner + 2 * n + 1, :, cols])
                    weights[coarse + s * n + t, :, cols] = value
                    store_pieces(coarse + s * n + t, group, value)
        for slot in range(sum(COUNTS), SLOTS):
            store_pieces(slot, group, jnp.zeros((K, 128), f32))

    flat_inverse = inverse.reshape(groups * SLOTS * ROWS, 128)
    column = lanes_of((8, 128)) % SEGMENT
    inside = ((gy > 0) | (column >= HALO)) & ((gy < lax.axis_size("gy") - 1) | (column < HALO + OWN))
    damped = jnp.where(inside, DAMPING, 0.0).astype(f32)
    half = K // 2
    tables = ((blocks, 0, COUNTS[0]), (coarse_blocks, COUNTS[0], SLOTS - COUNTS[0]))

    for group, (table, offset, count) in ((x, y) for x in range(groups) for y in tables):
        flat_blocks = table.reshape(groups * count * ROWS, 128)

        def multiply(g, group=group, table=table, offset=offset):
            for i in range(4):
                pair = jnp.dot(outer[...], pieces[group, offset // 2 + g * 4 + i], preferred_element_type=f32)
                table[group, g * 8 + 2 * i, pl.ds(0, K * K), :] = pair[:, :128]
                table[group, g * 8 + 2 * i + 1, pl.ds(0, K * K), :] = pair[:, 128:]

        def invert(g, carry, group=group, flat_blocks=flat_blocks, offset=offset, count=count, multiply=multiply):
            slot = offset + g * 8 + lax.broadcasted_iota(jnp.int32, (8, 128), 0)
            scale = jnp.where(
                slot < OFFSETS[1], 4.0, jnp.where(slot < OFFSETS[2], 8.0, jnp.where(slot < OFFSETS[3], 16.0, 32.0))
            ).astype(f32)
            source = (group * count + g * 8) * ROWS
            target = (group * SLOTS + offset + g * 8) * ROWS

            def load(k, l):
                value = flat_blocks[pl.ds(source + l * K + k, 8, stride=ROWS), :]
                return value + scale * prior_rows[pl.ds(k, 1), pl.ds(0, 128)] if k == l else value

            def store(k, l, value):
                value = value * damped
                flat_inverse[pl.ds(target + l * K + k, 8, stride=ROWS), :] = value
                if k != l:
                    flat_inverse[pl.ds(target + k * K + l, 8, stride=ROWS), :] = value

            for i in range(half):
                for j in range(half):
                    work[0, i * half + j] = load(half + j, i)
            for i in range(half):
                for j in range(i + 1):
                    work[2, i * half + j] = load(half + i, half + j)
            first = {(i, j): load(i, j) for i in range(half) for j in range(i + 1)}
            multiply(jnp.minimum(g + 1, count // 8 - 1))
            first = symmetric_inverse(first, half)
            for j in range(half):
                b = [work[0, i * half + j] for i in range(half)]
                for i in range(half):
                    work[1, i * half + j] = sum(first[max(i, h), min(i, h)] * b[h] for h in range(half))
            for i in range(half):
                for j in range(i + 1):
                    work[3, i * half + j] = first[i, j]
            schur = {(i, j): work[2, i * half + j] for i in range(half) for j in range(i + 1)}
            for h in range(half):
                b = [work[0, h * half + j] for j in range(half)]
                y = [work[1, h * half + j] for j in range(half)]
                for i in range(half):
                    for j in range(i + 1):
                        schur[i, j] = schur[i, j] - b[i] * y[j]
            second = symmetric_inverse(schur, half)
            for (i, j), value in second.items():
                store(half + i, half + j, value)
            for i in range(half):
                y = [work[1, i * half + j] for j in range(half)]
                for j in range(half):
                    z = sum(y[h] * second[max(h, j), min(h, j)] for h in range(half))
                    work[0, i * half + j] = z
                    store(half + j, i, -z)
            first = {(i, j): work[3, i * half + j] for i in range(half) for j in range(i + 1)}
            for h in range(half):
                z = [work[0, i * half + h] for i in range(half)]
                y = [work[1, i * half + h] for i in range(half)]
                for i in range(half):
                    for j in range(i + 1):
                        first[i, j] = first[i, j] + z[i] * y[j]
            for (i, j), value in first.items():
                store(i, j, value)
            return carry

        multiply(0)
        lax.fori_loop(0, count // 8, invert, 0)


def beside(read, m, s, t, above, below):
    n = SIDES[m]
    total = read(s - 1, t) if s > 0 else roll(read(n - 1, t), 1)
    total = total + (read(s + 1, t) if s < n - 1 else roll(read(0, t), -1))
    total = total + (read(s, t - 1) if t > 0 else jnp.where(above, roll(read(s, n - 1), SEGMENT), 0.0))
    return total + (read(s, t + 1) if t < n - 1 else jnp.where(below, roll(read(s, 0), -SEGMENT), 0.0))


def block_product(table, first, count, source, finish):
    def one(i, carry):
        for group in range(table.shape[0]):
            cols = pl.ds(group * 128, 128)
            total = None
            for l in range(K):
                term = table[group, first + i, pl.ds(l * K, K), :] * source[i, pl.ds(l, 1), cols]
                total = term if total is None else total + term
            finish(i, cols, total)
        return carry

    lax.fori_loop(0, count, one, 0, unroll=min(count, 16))


def v_cycle(inverse, prior, b, v, d, w):
    width = b[0].shape[-1]
    lane = lanes_of((K, width))
    above, below = lane >= SEGMENT, lane < width - SEGMENT
    weight = [prior[...] * 2.0**m for m in range(LEVELS)]

    def sweep(m, keep=None):
        n = SIDES[m]
        for s in range(n):
            for t in range(n):
                near = beside(lambda x, y: v[m][x * n + y], m, s, t, above, below)
                w[m][s * n + t] = b[m][s * n + t] + weight[m] * near

        def finish(i, cols, total):
            old = v[m][i, :, cols]
            v[m][i, :, cols] = 0.3 * old + total
            if keep is not None:
                keep[i, :, cols] = total - 0.4 * old

        block_product(inverse, OFFSETS[m], COUNTS[m], w[m], finish)

    def begin(m):
        def finish(i, cols, total):
            v[m][i, :, cols] = total

        block_product(inverse, OFFSETS[m], COUNTS[m], b[m], finish)

    for m in range(LEVELS - 1):
        n = SIDES[m]
        begin(m)
        sweep(m, d[m])
        for s in range(0, n, 2):
            for t in range(0, n, 2):
                near, own = None, None
                for x, y in ((s, t), (s, t + 1), (s + 1, t), (s + 1, t + 1)):
                    one = beside(lambda x, y: d[m][x * n + y], m, x, y, above, below)
                    near = one if near is None else near + one
                    one = b[m][x * n + y]
                    own = one if own is None else own + one
                b[m + 1][(s // 2) * (n // 2) + t // 2] = 0.09 * own + weight[m] * near
    begin(LEVELS - 1)
    for _ in range(COARSE_SWEEPS - 1):
        sweep(LEVELS - 1)
    for m in range(LEVELS - 2, -1, -1):
        n = SIDES[m]
        for s in range(n):
            for t in range(n):
                v[m][s * n + t] = v[m][s * n + t] + v[m + 1][(s // 2) * (n // 2) + t // 2]
        sweep(m)
        sweep(m)


def dots(rows, width, mine):
    totals = [jnp.zeros((K, width), f32) for _ in rows]
    for at in range(COUNTS[0]):
        for i, (one, other) in enumerate(rows):
            totals[i] = totals[i] + one[at] * other[at]
    lines = []
    for total in totals:
        total = jnp.sum(jnp.where(mine, total, 0.0), axis=0, keepdims=True)
        lines.append(sum(total[:, g * 128 : (g + 1) * 128] for g in range(width // 128)))
    if len(rows) % 8:
        lines.append(jnp.zeros((-len(rows) % 8, 128), f32))
    return jnp.concatenate(lines, axis=0)


def summed(sums):
    total = sums[0]
    for i in range(1, sums.shape[0]):
        total = total + sums[i]
    total = jnp.sum(total, axis=1, keepdims=True)
    return [total[i : i + 1] for i in range(total.shape[0])]


def best_factors(sums):
    values = summed(sums)
    lower, energy, row = {}, [], []
    for i in range(ITERS):
        cross = {}
        for j in range(i):
            cross[j] = values[GRAM.index((i, j))]
            for k in range(j):
                cross[j] = cross[j] - lower[j, k] * cross[k]
            lower[i, j] = cross[j] / energy[j]
        whole = values[GRAM.index((i, i))]
        left = whole
        for j in range(i):
            left = left - lower[i, j] * cross[j]
        energy.append(jnp.maximum(left, 1e-7 * whole))
        value = values[GRAM.index((i, -1))]
        for j in range(i):
            value = value - lower[i, j] * row[j]
        row.append(value)
    factors = [row[i] / energy[i] for i in range(ITERS)]
    for i in range(ITERS - 1, -1, -1):
        for j in range(i + 1, ITERS):
            factors[i] = factors[i] - lower[j, i] * factors[j]
    return [1.0 + factor for factor in factors]


def iterate_kernel(step, *refs):
    refs = list(refs)
    take = lambda n: [refs.pop(0) for _ in range(n)]
    last = step == ITERS - 1
    prior, blocks, inverse, residual = take(4)
    if step > 0:
        edge_a, edge_b, image = take(3)
    if last:
        earlier = [take(2) for _ in range(step)]
        sides = take(2)
        parts, packed, z, az, kept_residual, left_over = take(6)
    else:
        z, az, send_a, send_b = take(4)
        if step > 0:
            (left_over,) = take(1)
    b, v = ([one] + take(LEVELS - 1) for one in (left_over if step > 0 else residual, z))
    d, w = take(LEVELS - 1), take(LEVELS)
    width = z.shape[-1]
    lane = lanes_of((K, width))
    column = lane % SEGMENT
    mine = (column >= HALO) & (column < HALO + OWN)
    even = lax.axis_index("gy") % 2 == 0
    count = COUNTS[0]

    if step > 0:
        left_side, right_side = column < HALO, column >= HALO + OWN
        for i in range(count // 4):
            left = jnp.where(even, edge_b[i], edge_a[i])
            right = jnp.where(even, edge_a[i], edge_b[i])
            for g in range(4):
                at = 4 * i + g
                value = jnp.where(left_side, roll(left, -HALO * g), image[at])
                value = jnp.where(right_side, roll(right, SEGMENT - HALO - HALO * g), value)
                left_over[at] = residual[at] - value

    v_cycle(inverse, prior, b, v, d, w)

    above, below = lane >= SEGMENT, lane < width - SEGMENT
    weight = prior[...]
    n = SIDES[0]
    for s in range(n):
        for t in range(n):
            near = beside(lambda x, y: v[0][x * n + y], 0, s, t, above, below)
            w[0][s * n + t] = weight * (4.0 * v[0][s * n + t] - near)

    def finish(i, cols, total):
        value = total + w[0][i, :, cols]
        az[i, :, cols] = value
        if last:
            kept_residual[i, :, cols] = b[0][i, :, cols] - value

    block_product(blocks, 0, count, v[0], finish)

    if last:
        vectors = [one for one, _ in earlier] + [z]
        images = [one for _, one in earlier] + [az]
        pairs = [(z, one) for one in images] + [(one, kept_residual) for one in vectors]
        tile = dots(pairs, width, mine)
        first, second = sides[0][...], sides[1][...]
        row = lax.broadcasted_iota(jnp.int32, (8, 128), 0)
        other = jnp.where(row < 3, first, pltpu.roll(second, 3, 0))
        for i in range(parts.shape[0]):
            parts[i, pl.ds(0, 8), :] = tile
            parts[i, pl.ds(8, 8), :] = other
        pack(z, refs[-1], packed)
    else:
        for i in range(count // 4):
            left, right = None, None
            for g in range(4):
                value = az[4 * i + g]
                low, high = roll(value, HALO * g - HALO), roll(value, HALO * g - OWN)
                here = (column >= HALO * g) & (column < HALO * g + HALO)
                left = low if left is None else jnp.where(here, low, left)
                right = high if right is None else jnp.where(here, high, right)
            send_a[i] = jnp.where(even, right, left)
            send_b[i] = jnp.where(even, left, right)


def pack(source, tile, packed):
    gx = lax.axis_index("gx")
    group = pl.ds(pl.multiple_of((gx // 4) * 128, 128), 128)
    base = (gx % 4) * SEGMENT + HALO
    lane = lanes_of((K, 128))
    for t in range(BLOCK):
        row = None
        for s in range(BLOCK):
            value = pltpu.roll(source[s * BLOCK + t, :, group], (128 + s * OWN - base) % 128, 1)
            row = value if row is None else jnp.where(lane >= s * OWN, value, row)
        tile[pl.ds(t, K, stride=BLOCK), :] = row
    back = lax.dot_general(
        tile[...], lane_order(), (((1,), (1,)), ((), ())), precision=highest, preferred_element_type=f32
    )
    packed[...] = back.reshape(K, BLOCK, 128)


def side_kernel(step, *refs):
    fields, (out, *packed), tile = refs[: 2 * step + 2], refs[2 * step + 2 : -1], refs[-1]
    column = lanes_of(fields[0].shape[1:]) % SEGMENT
    mine = (column >= HALO) & (column < HALO + OWN)
    first = 0 if step == 1 else step
    pairs = [(fields[2 * i], fields[2 * j + 1]) for i in range(first, step + 1) for j in range(i + 1)]
    out[...] = dots(pairs, fields[0].shape[-1], mine)
    for i, target in enumerate(packed):
        pack(fields[2 * (first + i)], tile, target)


def finish_kernel(sums, *refs):
    packed, out = refs[:ITERS], refs[ITERS]
    factors = [jnp.broadcast_to(x, (BLOCK, 128)) for x in best_factors(sums)]
    for k in range(K):
        out[k] = sum(factors[i] * packed[i][k] for i in range(ITERS))


def gather(value):
    rows = lax.axis_size("gx")
    held = {0: value}
    bit = rows // 2
    while bit:
        pairs = [(i, i ^ bit) for i in range(rows)]
        for o in list(held):
            held[o ^ bit] = lax.ppermute(held[o], "gx", pairs)
        bit //= 2
    return [held[o] for o in range(rows)]


def local(beta, design, prior, kept, removed, removed_labels):
    rows, cols = lax.axis_size("gx"), lax.axis_size("gy")
    width = rows * SEGMENT
    pairs = [(i, i ^ 1) for i in range(cols)]
    others = [(0, 0)] + [(i, ((i + 1) ^ 1) - 1) for i in range(1, cols - 1)] + [(cols - 1, cols - 1)]
    others = others[1:-1]

    def shape(*dims, dtype=f32):
        return jax.ShapeDtypeStruct(dims, dtype)

    own, held, edge_a, edge_b, prior_rows = pl.pallas_call(
        prepare_kernel,
        out_shape=[shape(2, 8, K, 128)] * 2 + [shape(2, 4, K, 128)] * 2 + [shape(K, width)],
        in_specs=[SMEM, SMEM] + [VMEM] * 4,
        out_specs=[VMEM] * 5,
        scratch_shapes=[pltpu.VMEM((2 * K * BLOCK, 128), f32)],
        name="prepare",
    )(design, prior, beta, kept, removed, removed_labels)
    edge_a = lax.ppermute(edge_a, "gy", pairs)
    edge_b = lax.ppermute(edge_b, "gy", others)
    gathered = [held] + gather(own)[1:] + gather(edge_a) + gather(edge_b)

    products = (design[:, :, None] * design[:, None, :]).reshape(K, K * K).T
    parts, rest = [], products
    for _ in range(3):
        part = lax.reduce_precision(rest, 8, 7)
        parts.append(part)
        rest = rest - part
    outer = jnp.concatenate([parts[a] for a, _ in SPLITS], axis=1).astype(jnp.bfloat16)

    field = shape(COUNTS[0], K, width)
    blocks, inverse, rhs = pl.pallas_call(
        setup_kernel,
        out_shape=[shape(width // 128, n, ROWS, 128) for n in (COUNTS[0], SLOTS)] + [field],
        in_specs=[VMEM] * (2 + len(gathered)),
        out_specs=[VMEM] * 3,
        scratch_shapes=[
            pltpu.VMEM((SLOTS, K, width), f32),
            pltpu.VMEM((width // 128, SLOTS // 2, len(SPLITS) * K, 256), jnp.bfloat16),
            pltpu.VMEM((width // 128, SLOTS - COUNTS[0], ROWS, 128), f32),
            pltpu.VMEM((4, K * K // 4, 8, 128), f32),
        ],
        compiler_params=params(24 if width == 128 else 60),
        name="setup",
    )(outer, prior_rows, *gathered)

    levels = [pltpu.VMEM((n, K, width), f32) for n in COUNTS[1:] * 2 + COUNTS[:-1] + COUNTS]
    tile = pltpu.VMEM((K * BLOCK, 128), f32)
    own_tile = shape(*beta.shape)
    whole = pltpu.VMEM((COUNTS[0], K, width), f32)
    edge = shape(COUNTS[0] // 4, K, width)

    def iterate(step, *operands, shapes, scratch=()):
        return pl.pallas_call(
            functools.partial(iterate_kernel, step),
            out_shape=shapes,
            in_specs=[VMEM] * (len(operands) + 3),
            out_specs=[VMEM] * len(shapes),
            scratch_shapes=list(scratch[:4]) + levels + list(scratch[4:]),
            compiler_params=params(24 if width == 128 else 60),
            name=f"iterate_{step}",
        )(prior_rows, blocks, inverse, *operands)

    def exchange(edge_a, edge_b):
        return lax.ppermute(edge_a, "gy", pairs), lax.ppermute(edge_b, "gy", others)

    def total(parts):
        return lax.all_to_all(parts, "gy", 0, 0, tiled=True)

    residual, edges, image, earlier, sides, packed = rhs, (), (), (), (), ()
    for step in range(ITERS - 1):
        shapes = [field, field, edge, edge] + ([field] if step > 0 else [])
        z, az, *sent = iterate(step, residual, *edges, *image, shapes=shapes)
        edges, image, earlier = exchange(*sent[:2]), (az,), earlier + (z, az)
        if step > 0:
            residual = sent[2]
            fresh = [own_tile] * (2 if step == 1 else 1)
            side, *tiles = pl.pallas_call(
                functools.partial(side_kernel, step),
                out_shape=[shape(8, 128)] + fresh,
                in_specs=[VMEM] * len(earlier),
                out_specs=[VMEM] * (1 + len(fresh)),
                scratch_shapes=[tile],
                cost_estimate=pl.CostEstimate(flops=4_000_000, bytes_accessed=1_000_000, transcendentals=0),
                compiler_params=params(24 if width == 128 else 60),
                name=f"side_{step}",
            )(*earlier)
            sides, packed = sides + (side,), packed + tuple(tiles)
    parts, last_tile = iterate(
        ITERS - 1,
        residual,
        *edges,
        *image,
        *earlier,
        *sides,
        shapes=[shape(cols, 16, 128), own_tile],
        scratch=[whole] * 4 + [tile],
    )
    return pl.pallas_call(
        finish_kernel,
        out_shape=own_tile,
        in_specs=[VMEM] * (1 + ITERS),
        out_specs=VMEM,
        name="finish",
    )(total(parts), *packed, last_tile)


def solution(mesh):
    placed = (
        P(None, "gx", "gy"),
        P(),
        P(),
        P(None, "gx", "gy"),
        P(None, "gx", "gy"),
        P(None, "gx", "gy"),
    )
    return jax.shard_map(
        local, mesh=mesh, in_specs=placed, out_specs=P(None, "gx", "gy"), check_vma=False
    )
```

```python
import functools

import jax
import jax.numpy as jnp
from jax import lax
from jax.experimental import pallas as pl
from jax.experimental.pallas import tpu as pltpu
from jax.sharding import PartitionSpec as P

ITERS = 4
LEVELS = 4
COARSE_SWEEPS = 4
K = 16
BLOCK = 8
SEGMENT = 32
HALO = 8
OWN = 16
DAMPING = 0.7

highest = lax.Precision.HIGHEST
f32 = jnp.float32

SIDES = [BLOCK >> m for m in range(LEVELS)]
COUNTS = [n * n for n in SIDES]
OFFSETS = [sum(COUNTS[:m]) for m in range(LEVELS)]
SLOTS = -(-sum(COUNTS) // 8) * 8
ROWS = K * K + 8
GRAM = [(3, 0), (3, 1), (3, 2), (3, 3)] + [(i, -1) for i in range(ITERS)] + [(i, j) for i in range(3) for j in range(i + 1)]
SPLITS = ((0, 0), (0, 1), (0, 2), (1, 0), (1, 1), (2, 0))

VMEM = pl.BlockSpec(memory_space=pltpu.VMEM)
SMEM = pl.BlockSpec(memory_space=pltpu.SMEM)


def params(mib):
    return pltpu.CompilerParams(vmem_limit_bytes=mib << 20)


def lanes_of(shape):
    return lax.broadcasted_iota(jnp.int32, shape, len(shape) - 1)


def roll(x, shift):
    shift = shift % x.shape[-1]
    return x if shift == 0 else pltpu.roll(x, shift, x.ndim - 1)


def lane_order():
    row = lax.broadcasted_iota(jnp.int32, (128, 128), 0)
    lane = lax.broadcasted_iota(jnp.int32, (128, 128), 1)
    return (lane == (row % BLOCK) * OWN + row // BLOCK).astype(f32)


def prepare_kernel(design, beta, kept, removed, labels, own, edge_a, edge_b, tile):
    probs = []
    for j in range(K):
        logit = sum(design[j, k] * beta[k] for k in range(K))
        prob = 1.0 / (1.0 + jnp.exp(-logit))
        probs.append(removed[j].astype(f32) * prob - labels[j].astype(f32))
        tile[pl.ds(j * BLOCK, BLOCK), :] = kept[j].astype(f32) * prob * (1.0 - prob)
    for k in range(K):
        tile[pl.ds((K + k) * BLOCK, BLOCK), :] = sum(design[j, k] * probs[j] for j in range(K))
    tile[...] = jnp.dot(tile[...], lane_order(), precision=highest, preferred_element_type=f32)
    even = lax.axis_index("gy") % 2 == 0
    low = lanes_of((K, 128)) % OWN < HALO
    for f in range(2):
        rows = [tile[pl.ds(f * K * BLOCK + t, K, stride=BLOCK), :] for t in range(BLOCK)]
        for t in range(BLOCK):
            own[f, t] = rows[t]
        for i in range(BLOCK // 2):
            left = jnp.where(low, rows[2 * i], roll(rows[2 * i + 1], HALO))
            right = jnp.where(low, roll(rows[2 * i], -HALO), rows[2 * i + 1])
            edge_a[f, i] = jnp.where(even, right, left)
            edge_b[f, i] = jnp.where(even, left, right)


def hold_kernel(prior, own, held, prior_rows):
    held[...] = own[...]
    channel = lax.broadcasted_iota(jnp.int32, prior_rows.shape, 0)
    prior_rows[...] = sum(jnp.where(channel == k, prior[k], 0.0) for k in range(K))


def symmetric_inverse(a, n):
    a = dict(a)
    for p in range(n):
        d = 1.0 / a[p, p]
        col = {i: a[max(i, p), min(i, p)] for i in range(n) if i != p}
        fac = {i: col[i] * d for i in col}
        for i in col:
            for j in col:
                if j <= i:
                    a[i, j] = a[i, j] - fac[i] * col[j]
        for i in col:
            a[max(i, p), min(i, p)] = fac[i]
        a[p, p] = -d
    return {ij: -x for ij, x in a.items()}


def setup_kernel(outer, prior_rows, *refs):
    rows = (len(refs) - 7) // 3
    g_own, g_left, g_right = (refs[i * rows : (i + 1) * rows] for i in range(3))
    blocks, inverse, rhs, weights, pieces, coarse_blocks, work = refs[3 * rows :]
    gx, gy = lax.axis_index("gx"), lax.axis_index("gy")
    width = rhs.shape[-1]
    groups = width // 128
    lane = lanes_of((K, 128))
    even = gy % 2 == 0

    def store_pieces(slot, group, rest):
        cols = pl.ds((slot % 2) * 128, 128)
        parts = []
        for _ in range(3):
            part = rest.astype(jnp.bfloat16)
            parts.append(part)
            rest = rest - part.astype(f32)
        for i, (_, b) in enumerate(SPLITS):
            pieces[group, slot // 2, pl.ds(i * K, K), cols] = parts[b]

    for group in range(groups):
        bases = [(gx ^ o) * SEGMENT - group * 128 for o in range(rows)]
        masks = []
        for base in bases:
            at = lane - base
            masks.append(((at >= 0) & (at < HALO), (at >= HALO) & (at < HALO + OWN), (at >= HALO + OWN) & (at < SEGMENT)))
        for f in range(2):
            for t in range(BLOCK):
                own = [g_own[o][f, t] for o in range(rows)]
                first = [g_left[o][f, t // 2] for o in range(rows)]
                second = [g_right[o][f, t // 2] for o in range(rows)]
                left = [jnp.where(even, second[o], first[o]) for o in range(rows)]
                right = [jnp.where(even, first[o], second[o]) for o in range(rows)]
                odd = (t % 2) * HALO
                for s in range(BLOCK):
                    value = jnp.zeros((K, 128), f32)
                    for o in range(rows):
                        shift = bases[o] + 128 * rows - s * OWN
                        low, mid, high = masks[o]
                        value = jnp.where(low, pltpu.roll(left[o], (shift - odd) % 128, 1), value)
                        value = jnp.where(mid, pltpu.roll(own[o], (shift + HALO) % 128, 1), value)
                        value = jnp.where(high, pltpu.roll(right[o], (shift + SEGMENT - HALO - odd) % 128, 1), value)
                    if f == 0:
                        weights[s * BLOCK + t, :, pl.ds(group * 128, 128)] = value
                        store_pieces(s * BLOCK + t, group, value)
                    else:
                        rhs[s * BLOCK + t, :, pl.ds(group * 128, 128)] = value
        cols = pl.ds(group * 128, 128)
        for m in range(1, LEVELS):
            n, fine, coarse = SIDES[m], OFFSETS[m - 1], OFFSETS[m]
            for s in range(n):
                for t in range(n):
                    corner = fine + (2 * s) * (2 * n) + 2 * t
                    value = weights[corner, :, cols] + weights[corner + 1, :, cols]
                    value = value + (weights[corner + 2 * n, :, cols] + weights[corner + 2 * n + 1, :, cols])
                    weights[coarse + s * n + t, :, cols] = value
                    store_pieces(coarse + s * n + t, group, value)
        for slot in range(sum(COUNTS), SLOTS):
            store_pieces(slot, group, jnp.zeros((K, 128), f32))

    flat_inverse = inverse.reshape(groups * SLOTS * ROWS, 128)
    column = lanes_of((8, 128)) % SEGMENT
    inside = ((gy > 0) | (column >= HALO)) & ((gy < lax.axis_size("gy") - 1) | (column < HALO + OWN))
    damped = jnp.where(inside, DAMPING, 0.0).astype(f32)
    half = K // 2
    tables = ((blocks, 0, COUNTS[0]), (coarse_blocks, COUNTS[0], SLOTS - COUNTS[0]))

    for group, (table, offset, count) in ((x, y) for x in range(groups) for y in tables):
        flat_blocks = table.reshape(groups * count * ROWS, 128)

        def multiply(g, group=group, table=table, offset=offset):
            for i in range(4):
                pair = jnp.dot(outer[...], pieces[group, offset // 2 + g * 4 + i], preferred_element_type=f32)
                table[group, g * 8 + 2 * i, pl.ds(0, K * K), :] = pair[:, :128]
                table[group, g * 8 + 2 * i + 1, pl.ds(0, K * K), :] = pair[:, 128:]

        def invert(g, carry, group=group, flat_blocks=flat_blocks, offset=offset, count=count, multiply=multiply):
            slot = offset + g * 8 + lax.broadcasted_iota(jnp.int32, (8, 128), 0)
            scale = jnp.where(
                slot < OFFSETS[1], 4.0, jnp.where(slot < OFFSETS[2], 8.0, jnp.where(slot < OFFSETS[3], 16.0, 32.0))
            ).astype(f32)
            source = (group * count + g * 8) * ROWS
            target = (group * SLOTS + offset + g * 8) * ROWS

            def load(k, l):
                value = flat_blocks[pl.ds(source + l * K + k, 8, stride=ROWS), :]
                return value + scale * prior_rows[pl.ds(k, 1), pl.ds(0, 128)] if k == l else value

            def store(k, l, value):
                value = value * damped
                flat_inverse[pl.ds(target + l * K + k, 8, stride=ROWS), :] = value
                if k != l:
                    flat_inverse[pl.ds(target + k * K + l, 8, stride=ROWS), :] = value

            for i in range(half):
                for j in range(half):
                    work[0, i * half + j] = load(half + j, i)
            for i in range(half):
                for j in range(i + 1):
                    work[2, i * half + j] = load(half + i, half + j)
            first = {(i, j): load(i, j) for i in range(half) for j in range(i + 1)}
            multiply(jnp.minimum(g + 1, count // 8 - 1))
            first = symmetric_inverse(first, half)
            for j in range(half):
                b = [work[0, i * half + j] for i in range(half)]
                for i in range(half):
                    work[1, i * half + j] = sum(first[max(i, h), min(i, h)] * b[h] for h in range(half))
            for i in range(half):
                for j in range(i + 1):
                    work[3, i * half + j] = first[i, j]
            schur = {(i, j): work[2, i * half + j] for i in range(half) for j in range(i + 1)}
            for h in range(half):
                b = [work[0, h * half + j] for j in range(half)]
                y = [work[1, h * half + j] for j in range(half)]
                for i in range(half):
                    for j in range(i + 1):
                        schur[i, j] = schur[i, j] - b[i] * y[j]
            second = symmetric_inverse(schur, half)
            for (i, j), value in second.items():
                store(half + i, half + j, value)
            for i in range(half):
                y = [work[1, i * half + j] for j in range(half)]
                for j in range(half):
                    z = sum(y[h] * second[max(h, j), min(h, j)] for h in range(half))
                    work[0, i * half + j] = z
                    store(half + j, i, -z)
            first = {(i, j): work[3, i * half + j] for i in range(half) for j in range(i + 1)}
            for h in range(half):
                z = [work[0, i * half + h] for i in range(half)]
                y = [work[1, i * half + h] for i in range(half)]
                for i in range(half):
                    for j in range(i + 1):
                        first[i, j] = first[i, j] + z[i] * y[j]
            for (i, j), value in first.items():
                store(i, j, value)
            return carry

        multiply(0)
        lax.fori_loop(0, count // 8, invert, 0)


def beside(read, m, s, t, above, below):
    n = SIDES[m]
    total = read(s - 1, t) if s > 0 else roll(read(n - 1, t), 1)
    total = total + (read(s + 1, t) if s < n - 1 else roll(read(0, t), -1))
    total = total + (read(s, t - 1) if t > 0 else jnp.where(above, roll(read(s, n - 1), SEGMENT), 0.0))
    return total + (read(s, t + 1) if t < n - 1 else jnp.where(below, roll(read(s, 0), -SEGMENT), 0.0))


def block_product(table, first, count, source, finish):
    def one(i, carry):
        for group in range(table.shape[0]):
            cols = pl.ds(group * 128, 128)
            total = None
            for l in range(K):
                term = table[group, first + i, pl.ds(l * K, K), :] * source[i, pl.ds(l, 1), cols]
                total = term if total is None else total + term
            finish(i, cols, total)
        return carry

    lax.fori_loop(0, count, one, 0, unroll=min(count, 32))


def v_cycle(inverse, prior, b, v, d, w):
    width = b[0].shape[-1]
    lane = lanes_of((K, width))
    above, below = lane >= SEGMENT, lane < width - SEGMENT
    weight = [prior[...] * 2.0**m for m in range(LEVELS)]

    def sweep(m, keep=None):
        n = SIDES[m]
        for s in range(n):
            for t in range(n):
                near = beside(lambda x, y: v[m][x * n + y], m, s, t, above, below)
                w[m][s * n + t] = b[m][s * n + t] + weight[m] * near

        def finish(i, cols, total):
            old = v[m][i, :, cols]
            v[m][i, :, cols] = 0.3 * old + total
            if keep is not None:
                keep[i, :, cols] = total - 0.4 * old

        block_product(inverse, OFFSETS[m], COUNTS[m], w[m], finish)

    def begin(m):
        def finish(i, cols, total):
            v[m][i, :, cols] = total

        block_product(inverse, OFFSETS[m], COUNTS[m], b[m], finish)

    for m in range(LEVELS - 1):
        n = SIDES[m]
        begin(m)
        sweep(m, d[m])
        for s in range(0, n, 2):
            for t in range(0, n, 2):
                near, own = None, None
                for x, y in ((s, t), (s, t + 1), (s + 1, t), (s + 1, t + 1)):
                    one = beside(lambda x, y: d[m][x * n + y], m, x, y, above, below)
                    near = one if near is None else near + one
                    one = b[m][x * n + y]
                    own = one if own is None else own + one
                b[m + 1][(s // 2) * (n // 2) + t // 2] = 0.09 * own + weight[m] * near
    begin(LEVELS - 1)
    for _ in range(COARSE_SWEEPS - 1):
        sweep(LEVELS - 1)
    for m in range(LEVELS - 2, -1, -1):
        n = SIDES[m]
        for s in range(n):
            for t in range(n):
                v[m][s * n + t] = v[m][s * n + t] + v[m + 1][(s // 2) * (n // 2) + t // 2]
        sweep(m)
        sweep(m)


def dots(rows, width, mine):
    totals = [jnp.zeros((K, width), f32) for _ in rows]
    for at in range(COUNTS[0]):
        for i, (one, other) in enumerate(rows):
            totals[i] = totals[i] + one[at] * other[at]
    lines = []
    for total in totals:
        total = jnp.sum(jnp.where(mine, total, 0.0), axis=0, keepdims=True)
        lines.append(sum(total[:, g * 128 : (g + 1) * 128] for g in range(width // 128)))
    if len(rows) % 8:
        lines.append(jnp.zeros((-len(rows) % 8, 128), f32))
    return jnp.concatenate(lines, axis=0)


def summed(sums):
    total = sums[0]
    for i in range(1, sums.shape[0]):
        total = total + sums[i]
    total = jnp.sum(total, axis=1, keepdims=True)
    return [total[i : i + 1] for i in range(total.shape[0])]


def best_factors(sums):
    values = summed(sums)
    lower, energy, row = {}, [], []
    for i in range(ITERS):
        cross = {}
        for j in range(i):
            cross[j] = values[GRAM.index((i, j))]
            for k in range(j):
                cross[j] = cross[j] - lower[j, k] * cross[k]
            lower[i, j] = cross[j] / energy[j]
        whole = values[GRAM.index((i, i))]
        left = whole
        for j in range(i):
            left = left - lower[i, j] * cross[j]
        energy.append(jnp.maximum(left, 1e-7 * whole))
        value = values[GRAM.index((i, -1))]
        for j in range(i):
            value = value - lower[i, j] * row[j]
        row.append(value)
    factors = [row[i] / energy[i] for i in range(ITERS)]
    for i in range(ITERS - 1, -1, -1):
        for j in range(i + 1, ITERS):
            factors[i] = factors[i] - lower[j, i] * factors[j]
    return [1.0 + factor for factor in factors]


def iterate_kernel(step, *refs):
    refs = list(refs)
    take = lambda n: [refs.pop(0) for _ in range(n)]
    last = step == ITERS - 1
    prior, blocks, inverse, residual = take(4)
    if step > 0:
        edge_a, edge_b, image = take(3)
    if last:
        earlier = [take(2) for _ in range(step)]
        sides = take(2)
        parts, packed, z, az, kept_residual, left_over = take(6)
    else:
        z, az, send_a, send_b = take(4)
        if step > 0:
            (left_over,) = take(1)
    b, v = ([one] + take(LEVELS - 1) for one in (left_over if step > 0 else residual, z))
    d, w = take(LEVELS - 1), take(LEVELS)
    width = z.shape[-1]
    lane = lanes_of((K, width))
    column = lane % SEGMENT
    mine = (column >= HALO) & (column < HALO + OWN)
    even = lax.axis_index("gy") % 2 == 0
    count = COUNTS[0]

    if step > 0:
        left_side, right_side = column < HALO, column >= HALO + OWN
        for i in range(count // 4):
            left = jnp.where(even, edge_b[i], edge_a[i])
            right = jnp.where(even, edge_a[i], edge_b[i])
            for g in range(4):
                at = 4 * i + g
                value = jnp.where(left_side, roll(left, -HALO * g), image[at])
                value = jnp.where(right_side, roll(right, SEGMENT - HALO - HALO * g), value)
                left_over[at] = residual[at] - value

    v_cycle(inverse, prior, b, v, d, w)

    above, below = lane >= SEGMENT, lane < width - SEGMENT
    weight = prior[...]
    n = SIDES[0]
    for s in range(n):
        for t in range(n):
            near = beside(lambda x, y: v[0][x * n + y], 0, s, t, above, below)
            w[0][s * n + t] = weight * (4.0 * v[0][s * n + t] - near)

    def finish(i, cols, total):
        value = total + w[0][i, :, cols]
        az[i, :, cols] = value
        if last:
            kept_residual[i, :, cols] = b[0][i, :, cols] - value

    block_product(blocks, 0, count, v[0], finish)

    if last:
        vectors = [one for one, _ in earlier] + [z]
        images = [one for _, one in earlier] + [az]
        pairs = [(z, one) for one in images] + [(one, kept_residual) for one in vectors]
        tile = dots(pairs, width, mine)
        first, second = sides[0][...], sides[1][...]
        row = lax.broadcasted_iota(jnp.int32, (8, 128), 0)
        other = jnp.where(row < 3, first, pltpu.roll(second, 3, 0))
        for i in range(parts.shape[0]):
            parts[i, pl.ds(0, 8), :] = tile
            parts[i, pl.ds(8, 8), :] = other
        pack(z, refs[-1], packed)
    else:
        for i in range(count // 4):
            left, right = None, None
            for g in range(4):
                value = az[4 * i + g]
                low, high = roll(value, HALO * g - HALO), roll(value, HALO * g - OWN)
                here = (column >= HALO * g) & (column < HALO * g + HALO)
                left = low if left is None else jnp.where(here, low, left)
                right = high if right is None else jnp.where(here, high, right)
            send_a[i] = jnp.where(even, right, left)
            send_b[i] = jnp.where(even, left, right)


def pack(source, tile, packed):
    gx = lax.axis_index("gx")
    group = pl.ds(pl.multiple_of((gx // 4) * 128, 128), 128)
    base = (gx % 4) * SEGMENT + HALO
    lane = lanes_of((K, 128))
    for t in range(BLOCK):
        row = None
        for s in range(BLOCK):
            value = pltpu.roll(source[s * BLOCK + t, :, group], (128 + s * OWN - base) % 128, 1)
            row = value if row is None else jnp.where(lane >= s * OWN, value, row)
        tile[pl.ds(t, K, stride=BLOCK), :] = row
    back = lax.dot_general(
        tile[...], lane_order(), (((1,), (1,)), ((), ())), precision=highest, preferred_element_type=f32
    )
    packed[...] = back.reshape(K, BLOCK, 128)


def side_kernel(step, *refs):
    fields, (out, *packed), tile = refs[: 2 * step + 2], refs[2 * step + 2 : -1], refs[-1]
    column = lanes_of(fields[0].shape[1:]) % SEGMENT
    mine = (column >= HALO) & (column < HALO + OWN)
    first = 0 if step == 1 else step
    pairs = [(fields[2 * i], fields[2 * j + 1]) for i in range(first, step + 1) for j in range(i + 1)]
    out[...] = dots(pairs, fields[0].shape[-1], mine)
    for i, target in enumerate(packed):
        pack(fields[2 * (first + i)], tile, target)


def finish_kernel(sums, *refs):
    packed, out = refs[:ITERS], refs[ITERS]
    factors = [jnp.broadcast_to(x, (BLOCK, 128)) for x in best_factors(sums)]
    for k in range(K):
        out[k] = sum(factors[i] * packed[i][k] for i in range(ITERS))


def gather(value, beside=None):
    rows = lax.axis_size("gx")
    held = {0: value}
    bit = rows // 2
    while bit:
        pairs = [(i, i ^ bit) for i in range(rows)]
        for o in list(held):
            held[o ^ bit] = lax.ppermute(held[o], "gx", pairs)
        if beside is not None:
            *beside, held[bit] = lax.optimization_barrier((*beside, held[bit]))
        bit //= 2
    values = [held[o] for o in range(rows)]
    return values if beside is None else (values, beside)


def local(beta, design, prior, kept, removed, removed_labels):
    rows, cols = lax.axis_size("gx"), lax.axis_size("gy")
    width = rows * SEGMENT
    pairs = [(i, i ^ 1) for i in range(cols)]
    others = [(0, 0)] + [(i, ((i + 1) ^ 1) - 1) for i in range(1, cols - 1)] + [(cols - 1, cols - 1)]
    others = others[1:-1]

    def shape(*dims, dtype=f32):
        return jax.ShapeDtypeStruct(dims, dtype)

    own, edge_a, edge_b = pl.pallas_call(
        prepare_kernel,
        out_shape=[shape(2, 8, K, 128)] + [shape(2, 4, K, 128)] * 2,
        in_specs=[SMEM] + [VMEM] * 4,
        out_specs=[VMEM] * 3,
        scratch_shapes=[pltpu.VMEM((2 * K * BLOCK, 128), f32)],
        name="prepare",
    )(design, beta, kept, removed, removed_labels)
    held, prior_rows = pl.pallas_call(
        hold_kernel,
        out_shape=[shape(*own.shape), shape(K, width)],
        in_specs=[SMEM, VMEM],
        out_specs=[VMEM] * 2,
        compiler_params=params(24),
        name="hold",
    )(prior, own)
    edge_a = lax.ppermute(edge_a, "gy", pairs)
    edge_b = lax.ppermute(edge_b, "gy", others)
    last, (held, prior_rows) = gather(edge_b, (held, prior_rows))
    gathered = [held] + gather(own)[1:] + gather(edge_a) + last

    products = (design[:, :, None] * design[:, None, :]).reshape(K, K * K).T
    parts, rest = [], products
    for _ in range(3):
        part = lax.reduce_precision(rest, 8, 7)
        parts.append(part)
        rest = rest - part
    outer = jnp.concatenate([parts[a] for a, _ in SPLITS], axis=1).astype(jnp.bfloat16)

    field = shape(COUNTS[0], K, width)
    blocks, inverse, rhs = pl.pallas_call(
        setup_kernel,
        out_shape=[shape(width // 128, n, ROWS, 128) for n in (COUNTS[0], SLOTS)] + [field],
        in_specs=[VMEM] * (2 + len(gathered)),
        out_specs=[VMEM] * 3,
        scratch_shapes=[
            pltpu.VMEM((SLOTS, K, width), f32),
            pltpu.VMEM((width // 128, SLOTS // 2, len(SPLITS) * K, 256), jnp.bfloat16),
            pltpu.VMEM((width // 128, SLOTS - COUNTS[0], ROWS, 128), f32),
            pltpu.VMEM((4, K * K // 4, 8, 128), f32),
        ],
        compiler_params=params(24 if width == 128 else 60),
        name="setup",
    )(outer, prior_rows, *gathered)

    levels = [pltpu.VMEM((n, K, width), f32) for n in COUNTS[1:] * 2 + COUNTS[:-1] + COUNTS]
    tile = pltpu.VMEM((K * BLOCK, 128), f32)
    own_tile = shape(*beta.shape)
    whole = pltpu.VMEM((COUNTS[0], K, width), f32)
    edge = shape(COUNTS[0] // 4, K, width)

    def iterate(step, *operands, shapes, scratch=()):
        return pl.pallas_call(
            functools.partial(iterate_kernel, step),
            out_shape=shapes,
            in_specs=[VMEM] * (len(operands) + 3),
            out_specs=[VMEM] * len(shapes),
            scratch_shapes=list(scratch[:4]) + levels + list(scratch[4:]),
            compiler_params=params(24 if width == 128 else 60),
            name=f"iterate_{step}",
        )(prior_rows, blocks, inverse, *operands)

    def exchange(edge_a, edge_b):
        return lax.ppermute(edge_a, "gy", pairs), lax.ppermute(edge_b, "gy", others)

    def total(parts):
        return lax.all_to_all(parts, "gy", 0, 0, tiled=True)

    residual, edges, image, earlier, sides, packed = rhs, (), (), (), (), ()
    for step in range(ITERS - 1):
        shapes = [field, field, edge, edge] + ([field] if step > 0 else [])
        z, az, *sent = iterate(step, residual, *edges, *image, shapes=shapes)
        edges, image, earlier = exchange(*sent[:2]), (az,), earlier + (z, az)
        if step > 0:
            residual = sent[2]
            fresh = [own_tile] * (2 if step == 1 else 1)
            side, *tiles = pl.pallas_call(
                functools.partial(side_kernel, step),
                out_shape=[shape(8, 128)] + fresh,
                in_specs=[VMEM] * len(earlier),
                out_specs=[VMEM] * (1 + len(fresh)),
                scratch_shapes=[tile],
                cost_estimate=pl.CostEstimate(flops=4_000_000, bytes_accessed=1_000_000, transcendentals=0),
                compiler_params=params(24 if width == 128 else 60),
                name=f"side_{step}",
            )(*earlier)
            sides, packed = sides + (side,), packed + tuple(tiles)
    parts, last_tile = iterate(
        ITERS - 1,
        residual,
        *edges,
        *image,
        *earlier,
        *sides,
        shapes=[shape(cols, 16, 128), own_tile],
        scratch=[whole] * 4 + [tile],
    )
    return pl.pallas_call(
        finish_kernel,
        out_shape=own_tile,
        in_specs=[VMEM] * (1 + ITERS),
        out_specs=VMEM,
        compiler_params=params(8),
        name="finish",
    )(total(parts), *packed, last_tile)


def solution(mesh):
    placed = (
        P(None, "gx", "gy"),
        P(),
        P(),
        P(None, "gx", "gy"),
        P(None, "gx", "gy"),
        P(None, "gx", "gy"),
    )
    return jax.shard_map(
        local, mesh=mesh, in_specs=placed, out_specs=P(None, "gx", "gy"), check_vma=False
    )
```

```python
import functools

import jax
import jax.numpy as jnp
from jax import lax
from jax.experimental import pallas as pl
from jax.experimental.pallas import tpu as pltpu
from jax.sharding import PartitionSpec as P

ITERS = 4
LEVELS = 4
COARSE_SWEEPS = 4
K = 16
BLOCK = 8
SEGMENT = 32
HALO = 8
OWN = 16
DAMPING = 0.7

highest = lax.Precision.HIGHEST
f32 = jnp.float32

SIDES = [BLOCK >> m for m in range(LEVELS)]
COUNTS = [n * n for n in SIDES]
OFFSETS = [sum(COUNTS[:m]) for m in range(LEVELS)]
SLOTS = -(-sum(COUNTS) // 8) * 8
ROWS = K * K + 8
GRAM = [(3, 0), (3, 1), (3, 2), (3, 3)] + [(i, -1) for i in range(ITERS)] + [(i, j) for i in range(3) for j in range(i + 1)]
SPLITS = ((0, 0), (0, 1), (0, 2), (1, 0), (1, 1), (2, 0))

VMEM = pl.BlockSpec(memory_space=pltpu.VMEM)
SMEM = pl.BlockSpec(memory_space=pltpu.SMEM)


def params(mib):
    return pltpu.CompilerParams(vmem_limit_bytes=mib << 20)


def lanes_of(shape):
    return lax.broadcasted_iota(jnp.int32, shape, len(shape) - 1)


def roll(x, shift):
    shift = shift % x.shape[-1]
    return x if shift == 0 else pltpu.roll(x, shift, x.ndim - 1)


def lane_order():
    row = lax.broadcasted_iota(jnp.int32, (128, 128), 0)
    lane = lax.broadcasted_iota(jnp.int32, (128, 128), 1)
    return (lane == (row % BLOCK) * OWN + row // BLOCK).astype(f32)


def prepare_kernel(design, beta, kept, removed, labels, own, edge_a, edge_b, tile):
    probs = []
    for j in range(K):
        logit = sum(design[j, k] * beta[k] for k in range(K))
        prob = 1.0 / (1.0 + jnp.exp(-logit))
        probs.append(removed[j].astype(f32) * prob - labels[j].astype(f32))
        tile[pl.ds(j * BLOCK, BLOCK), :] = kept[j].astype(f32) * prob * (1.0 - prob)
    for k in range(K):
        tile[pl.ds((K + k) * BLOCK, BLOCK), :] = sum(design[j, k] * probs[j] for j in range(K))
    tile[...] = jnp.dot(tile[...], lane_order(), precision=highest, preferred_element_type=f32)
    even = lax.axis_index("gy") % 2 == 0
    low = lanes_of((K, 128)) % OWN < HALO
    for f in range(2):
        rows = [tile[pl.ds(f * K * BLOCK + t, K, stride=BLOCK), :] for t in range(BLOCK)]
        for t in range(BLOCK):
            own[f, t] = rows[t]
        for i in range(BLOCK // 2):
            left = jnp.where(low, rows[2 * i], roll(rows[2 * i + 1], HALO))
            right = jnp.where(low, roll(rows[2 * i], -HALO), rows[2 * i + 1])
            edge_a[f, i] = jnp.where(even, right, left)
            edge_b[f, i] = jnp.where(even, left, right)


def hold_kernel(prior, own, held, prior_rows):
    held[...] = own[...]
    channel = lax.broadcasted_iota(jnp.int32, prior_rows.shape, 0)
    prior_rows[...] = sum(jnp.where(channel == k, prior[k], 0.0) for k in range(K))


def symmetric_inverse(a, n):
    a = dict(a)
    for p in range(n):
        d = 1.0 / a[p, p]
        col = {i: a[max(i, p), min(i, p)] for i in range(n) if i != p}
        fac = {i: col[i] * d for i in col}
        for i in col:
            for j in col:
                if j <= i:
                    a[i, j] = a[i, j] - fac[i] * col[j]
        for i in col:
            a[max(i, p), min(i, p)] = fac[i]
        a[p, p] = -d
    return {ij: -x for ij, x in a.items()}


def setup_kernel(outer, prior_rows, *refs):
    rows = (len(refs) - 7) // 3
    g_own, g_left, g_right = (refs[i * rows : (i + 1) * rows] for i in range(3))
    blocks, inverse, rhs, weights, pieces, coarse_blocks, work = refs[3 * rows :]
    gx, gy = lax.axis_index("gx"), lax.axis_index("gy")
    width = rhs.shape[-1]
    groups = width // 128
    lane = lanes_of((K, 128))
    even = gy % 2 == 0

    def store_pieces(slot, group, rest):
        cols = pl.ds((slot % 2) * 128, 128)
        parts = []
        for _ in range(3):
            part = rest.astype(jnp.bfloat16)
            parts.append(part)
            rest = rest - part.astype(f32)
        for i, (_, b) in enumerate(SPLITS):
            pieces[group, slot // 2, pl.ds(i * K, K), cols] = parts[b]

    for group in range(groups):
        bases = [(gx ^ o) * SEGMENT - group * 128 for o in range(rows)]
        masks = []
        for base in bases:
            at = lane - base
            masks.append(((at >= 0) & (at < HALO), (at >= HALO) & (at < HALO + OWN), (at >= HALO + OWN) & (at < SEGMENT)))
        for f in range(2):
            for t in range(BLOCK):
                own = [g_own[o][f, t] for o in range(rows)]
                first = [g_left[o][f, t // 2] for o in range(rows)]
                second = [g_right[o][f, t // 2] for o in range(rows)]
                left = [jnp.where(even, second[o], first[o]) for o in range(rows)]
                right = [jnp.where(even, first[o], second[o]) for o in range(rows)]
                odd = (t % 2) * HALO
                for s in range(BLOCK):
                    value = jnp.zeros((K, 128), f32)
                    for o in range(rows):
                        shift = bases[o] + 128 * rows - s * OWN
                        low, mid, high = masks[o]
                        value = jnp.where(low, pltpu.roll(left[o], (shift - odd) % 128, 1), value)
                        value = jnp.where(mid, pltpu.roll(own[o], (shift + HALO) % 128, 1), value)
                        value = jnp.where(high, pltpu.roll(right[o], (shift + SEGMENT - HALO - odd) % 128, 1), value)
                    if f == 0:
                        weights[s * BLOCK + t, :, pl.ds(group * 128, 128)] = value
                        store_pieces(s * BLOCK + t, group, value)
                    else:
                        rhs[s * BLOCK + t, :, pl.ds(group * 128, 128)] = value
        cols = pl.ds(group * 128, 128)
        for m in range(1, LEVELS):
            n, fine, coarse = SIDES[m], OFFSETS[m - 1], OFFSETS[m]
            for s in range(n):
                for t in range(n):
                    corner = fine + (2 * s) * (2 * n) + 2 * t
                    value = weights[corner, :, cols] + weights[corner + 1, :, cols]
                    value = value + (weights[corner + 2 * n, :, cols] + weights[corner + 2 * n + 1, :, cols])
                    weights[coarse + s * n + t, :, cols] = value
                    store_pieces(coarse + s * n + t, group, value)
        for slot in range(sum(COUNTS), SLOTS):
            store_pieces(slot, group, jnp.zeros((K, 128), f32))

    flat_inverse = inverse.reshape(groups * SLOTS * ROWS, 128)
    column = lanes_of((8, 128)) % SEGMENT
    inside = ((gy > 0) | (column >= HALO)) & ((gy < lax.axis_size("gy") - 1) | (column < HALO + OWN))
    damped = jnp.where(inside, DAMPING, 0.0).astype(f32)
    half = K // 2
    tables = ((blocks, 0, COUNTS[0]), (coarse_blocks, COUNTS[0], SLOTS - COUNTS[0]))

    for group, (table, offset, count) in ((x, y) for x in range(groups) for y in tables):
        flat_blocks = table.reshape(groups * count * ROWS, 128)

        def multiply(g, group=group, table=table, offset=offset):
            for i in range(4):
                pair = jnp.dot(outer[...], pieces[group, offset // 2 + g * 4 + i], preferred_element_type=f32)
                table[group, g * 8 + 2 * i, pl.ds(0, K * K), :] = pair[:, :128]
                table[group, g * 8 + 2 * i + 1, pl.ds(0, K * K), :] = pair[:, 128:]

        def invert(g, carry, group=group, flat_blocks=flat_blocks, offset=offset, count=count, multiply=multiply):
            slot = offset + g * 8 + lax.broadcasted_iota(jnp.int32, (8, 128), 0)
            scale = jnp.where(
                slot < OFFSETS[1], 4.0, jnp.where(slot < OFFSETS[2], 8.0, jnp.where(slot < OFFSETS[3], 16.0, 32.0))
            ).astype(f32)
            source = (group * count + g * 8) * ROWS
            target = (group * SLOTS + offset + g * 8) * ROWS

            def load(k, l):
                value = flat_blocks[pl.ds(source + l * K + k, 8, stride=ROWS), :]
                return value + scale * prior_rows[pl.ds(k, 1), pl.ds(0, 128)] if k == l else value

            def store(k, l, value):
                value = value * damped
                flat_inverse[pl.ds(target + l * K + k, 8, stride=ROWS), :] = value
                if k != l:
                    flat_inverse[pl.ds(target + k * K + l, 8, stride=ROWS), :] = value

            for i in range(half):
                for j in range(half):
                    work[0, i * half + j] = load(half + j, i)
            for i in range(half):
                for j in range(i + 1):
                    work[2, i * half + j] = load(half + i, half + j)
            first = {(i, j): load(i, j) for i in range(half) for j in range(i + 1)}
            multiply(jnp.minimum(g + 1, count // 8 - 1))
            first = symmetric_inverse(first, half)
            for j in range(half):
                b = [work[0, i * half + j] for i in range(half)]
                for i in range(half):
                    work[1, i * half + j] = sum(first[max(i, h), min(i, h)] * b[h] for h in range(half))
            for i in range(half):
                for j in range(i + 1):
                    work[3, i * half + j] = first[i, j]
            schur = {(i, j): work[2, i * half + j] for i in range(half) for j in range(i + 1)}
            for h in range(half):
                b = [work[0, h * half + j] for j in range(half)]
                y = [work[1, h * half + j] for j in range(half)]
                for i in range(half):
                    for j in range(i + 1):
                        schur[i, j] = schur[i, j] - b[i] * y[j]
            second = symmetric_inverse(schur, half)
            for (i, j), value in second.items():
                store(half + i, half + j, value)
            for i in range(half):
                y = [work[1, i * half + j] for j in range(half)]
                for j in range(half):
                    z = sum(y[h] * second[max(h, j), min(h, j)] for h in range(half))
                    work[0, i * half + j] = z
                    store(half + j, i, -z)
            first = {(i, j): work[3, i * half + j] for i in range(half) for j in range(i + 1)}
            for h in range(half):
                z = [work[0, i * half + h] for i in range(half)]
                y = [work[1, i * half + h] for i in range(half)]
                for i in range(half):
                    for j in range(i + 1):
                        first[i, j] = first[i, j] + z[i] * y[j]
            for (i, j), value in first.items():
                store(i, j, value)
            return carry

        multiply(0)
        lax.fori_loop(0, count // 8, invert, 0)


def beside(read, m, s, t, above, below):
    n = SIDES[m]
    total = read(s - 1, t) if s > 0 else roll(read(n - 1, t), 1)
    total = total + (read(s + 1, t) if s < n - 1 else roll(read(0, t), -1))
    total = total + (read(s, t - 1) if t > 0 else jnp.where(above, roll(read(s, n - 1), SEGMENT), 0.0))
    return total + (read(s, t + 1) if t < n - 1 else jnp.where(below, roll(read(s, 0), -SEGMENT), 0.0))


def block_product(table, first, count, source, finish):
    def one(i, carry):
        for group in range(table.shape[0]):
            cols = pl.ds(group * 128, 128)
            total = None
            for l in range(K):
                term = table[group, first + i, pl.ds(l * K, K), :] * source[i, pl.ds(l, 1), cols]
                total = term if total is None else total + term
            finish(i, cols, total)
        return carry

    lax.fori_loop(0, count, one, 0, unroll=min(count, 32))


def v_cycle(inverse, prior, b, v, d, w):
    width = b[0].shape[-1]
    lane = lanes_of((K, width))
    above, below = lane >= SEGMENT, lane < width - SEGMENT
    weight = [prior[...] * 2.0**m for m in range(LEVELS)]

    def sweep(m, keep=None):
        n = SIDES[m]
        for s in range(n):
            for t in range(n):
                near = beside(lambda x, y: v[m][x * n + y], m, s, t, above, below)
                w[m][s * n + t] = b[m][s * n + t] + weight[m] * near

        def finish(i, cols, total):
            old = v[m][i, :, cols]
            v[m][i, :, cols] = 0.3 * old + total
            if keep is not None:
                keep[i, :, cols] = total - 0.4 * old

        block_product(inverse, OFFSETS[m], COUNTS[m], w[m], finish)

    def begin(m):
        def finish(i, cols, total):
            v[m][i, :, cols] = total

        block_product(inverse, OFFSETS[m], COUNTS[m], b[m], finish)

    for m in range(LEVELS - 1):
        n = SIDES[m]
        begin(m)
        sweep(m, d[m])
        for s in range(0, n, 2):
            for t in range(0, n, 2):
                near, own = None, None
                for x, y in ((s, t), (s, t + 1), (s + 1, t), (s + 1, t + 1)):
                    one = beside(lambda x, y: d[m][x * n + y], m, x, y, above, below)
                    near = one if near is None else near + one
                    one = b[m][x * n + y]
                    own = one if own is None else own + one
                b[m + 1][(s // 2) * (n // 2) + t // 2] = 0.09 * own + weight[m] * near
    begin(LEVELS - 1)
    for _ in range(COARSE_SWEEPS - 1):
        sweep(LEVELS - 1)
    for m in range(LEVELS - 2, -1, -1):
        n = SIDES[m]
        for s in range(n):
            for t in range(n):
                v[m][s * n + t] = v[m][s * n + t] + v[m + 1][(s // 2) * (n // 2) + t // 2]
        sweep(m)
        sweep(m)


def dots(rows, width, mine):
    totals = [jnp.zeros((K, width), f32) for _ in rows]
    for at in range(COUNTS[0]):
        for i, (one, other) in enumerate(rows):
            totals[i] = totals[i] + one[at] * other[at]
    lines = []
    for total in totals:
        total = jnp.sum(jnp.where(mine, total, 0.0), axis=0, keepdims=True)
        lines.append(sum(total[:, g * 128 : (g + 1) * 128] for g in range(width // 128)))
    if len(rows) % 8:
        lines.append(jnp.zeros((-len(rows) % 8, 128), f32))
    return jnp.concatenate(lines, axis=0)


def summed(sums):
    total = sums[0]
    for i in range(1, sums.shape[0]):
        total = total + sums[i]
    total = jnp.sum(total, axis=1, keepdims=True)
    return [total[i : i + 1] for i in range(total.shape[0])]


def best_factors(sums):
    values = summed(sums)
    lower, energy, row = {}, [], []
    for i in range(ITERS):
        cross = {}
        for j in range(i):
            cross[j] = values[GRAM.index((i, j))]
            for k in range(j):
                cross[j] = cross[j] - lower[j, k] * cross[k]
            lower[i, j] = cross[j] / energy[j]
        whole = values[GRAM.index((i, i))]
        left = whole
        for j in range(i):
            left = left - lower[i, j] * cross[j]
        energy.append(jnp.maximum(left, 1e-7 * whole))
        value = values[GRAM.index((i, -1))]
        for j in range(i):
            value = value - lower[i, j] * row[j]
        row.append(value)
    factors = [row[i] / energy[i] for i in range(ITERS)]
    for i in range(ITERS - 1, -1, -1):
        for j in range(i + 1, ITERS):
            factors[i] = factors[i] - lower[j, i] * factors[j]
    return [1.0 + factor for factor in factors]


def iterate_kernel(step, *refs):
    refs = list(refs)
    take = lambda n: [refs.pop(0) for _ in range(n)]
    last = step == ITERS - 1
    prior, blocks, inverse, residual = take(4)
    if step > 0:
        edge_a, edge_b, image = take(3)
    if last:
        earlier = [take(2) for _ in range(step)]
        sides = take(2)
        parts, packed, z, az, kept_residual, left_over = take(6)
    else:
        z, az, send_a, send_b = take(4)
        if step > 0:
            (left_over,) = take(1)
    b, v = ([one] + take(LEVELS - 1) for one in (left_over if step > 0 else residual, z))
    d, w = take(LEVELS - 1), take(LEVELS)
    width = z.shape[-1]
    lane = lanes_of((K, width))
    column = lane % SEGMENT
    mine = (column >= HALO) & (column < HALO + OWN)
    even = lax.axis_index("gy") % 2 == 0
    count = COUNTS[0]

    if step > 0:
        left_side, right_side = column < HALO, column >= HALO + OWN
        for i in range(count // 4):
            left = jnp.where(even, edge_b[i], edge_a[i])
            right = jnp.where(even, edge_a[i], edge_b[i])
            for g in range(4):
                at = 4 * i + g
                value = jnp.where(left_side, roll(left, -HALO * g), image[at])
                value = jnp.where(right_side, roll(right, SEGMENT - HALO - HALO * g), value)
                left_over[at] = residual[at] - value

    v_cycle(inverse, prior, b, v, d, w)

    above, below = lane >= SEGMENT, lane < width - SEGMENT
    weight = prior[...]
    n = SIDES[0]
    for s in range(n):
        for t in range(n):
            near = beside(lambda x, y: v[0][x * n + y], 0, s, t, above, below)
            w[0][s * n + t] = weight * (4.0 * v[0][s * n + t] - near)

    def finish(i, cols, total):
        value = total + w[0][i, :, cols]
        az[i, :, cols] = value
        if last:
            kept_residual[i, :, cols] = b[0][i, :, cols] - value

    block_product(blocks, 0, count, v[0], finish)

    if last:
        vectors = [one for one, _ in earlier] + [z]
        images = [one for _, one in earlier] + [az]
        pairs = [(z, one) for one in images] + [(one, kept_residual) for one in vectors]
        tile = dots(pairs, width, mine)
        first, second = sides[0][...], sides[1][...]
        row = lax.broadcasted_iota(jnp.int32, (8, 128), 0)
        other = jnp.where(row < 3, first, pltpu.roll(second, 3, 0))
        for i in range(parts.shape[0]):
            parts[i, pl.ds(0, 8), :] = tile
            parts[i, pl.ds(8, 8), :] = other
        pack(z, refs[-1], packed)
    else:
        for i in range(count // 4):
            left, right = None, None
            for g in range(4):
                value = az[4 * i + g]
                low, high = roll(value, HALO * g - HALO), roll(value, HALO * g - OWN)
                here = (column >= HALO * g) & (column < HALO * g + HALO)
                left = low if left is None else jnp.where(here, low, left)
                right = high if right is None else jnp.where(here, high, right)
            send_a[i] = jnp.where(even, right, left)
            send_b[i] = jnp.where(even, left, right)


def pack(source, tile, packed):
    gx = lax.axis_index("gx")
    group = pl.ds(pl.multiple_of((gx // 4) * 128, 128), 128)
    base = (gx % 4) * SEGMENT + HALO
    lane = lanes_of((K, 128))
    for t in range(BLOCK):
        row = None
        for s in range(BLOCK):
            value = pltpu.roll(source[s * BLOCK + t, :, group], (128 + s * OWN - base) % 128, 1)
            row = value if row is None else jnp.where(lane >= s * OWN, value, row)
        tile[pl.ds(t, K, stride=BLOCK), :] = row
    back = lax.dot_general(
        tile[...], lane_order(), (((1,), (1,)), ((), ())), precision=highest, preferred_element_type=f32
    )
    packed[...] = back.reshape(K, BLOCK, 128)


def side_kernel(step, *refs):
    fields, (out, *packed), tile = refs[: 2 * step + 2], refs[2 * step + 2 : -1], refs[-1]
    column = lanes_of(fields[0].shape[1:]) % SEGMENT
    mine = (column >= HALO) & (column < HALO + OWN)
    first = 0 if step == 1 else step
    pairs = [(fields[2 * i], fields[2 * j + 1]) for i in range(first, step + 1) for j in range(i + 1)]
    out[...] = dots(pairs, fields[0].shape[-1], mine)
    for i, target in enumerate(packed):
        pack(fields[2 * (first + i)], tile, target)


def finish_kernel(sums, *refs):
    packed, out = refs[:ITERS], refs[ITERS]
    factors = [jnp.broadcast_to(x, (BLOCK, 128)) for x in best_factors(sums)]
    for k in range(K):
        out[k] = sum(factors[i] * packed[i][k] for i in range(ITERS))


def gather(value, beside=None):
    rows = lax.axis_size("gx")
    held = {0: value}
    bit = rows // 2
    while bit:
        pairs = [(i, i ^ bit) for i in range(rows)]
        for o in list(held):
            held[o ^ bit] = lax.ppermute(held[o], "gx", pairs)
        if beside is not None:
            *beside, held[bit] = lax.optimization_barrier((*beside, held[bit]))
        bit //= 2
    values = [held[o] for o in range(rows)]
    return values if beside is None else (values, beside)


def local(beta, design, prior, kept, removed, removed_labels):
    rows, cols = lax.axis_size("gx"), lax.axis_size("gy")
    width = rows * SEGMENT
    pairs = [(i, i ^ 1) for i in range(cols)]
    others = [(0, 0)] + [(i, ((i + 1) ^ 1) - 1) for i in range(1, cols - 1)] + [(cols - 1, cols - 1)]
    others = others[1:-1]

    def shape(*dims, dtype=f32):
        return jax.ShapeDtypeStruct(dims, dtype)

    own, edge_a, edge_b = pl.pallas_call(
        prepare_kernel,
        out_shape=[shape(2, 8, K, 128)] + [shape(2, 4, K, 128)] * 2,
        in_specs=[SMEM] + [VMEM] * 4,
        out_specs=[VMEM] * 3,
        scratch_shapes=[pltpu.VMEM((2 * K * BLOCK, 128), f32)],
        name="prepare",
    )(design, beta, kept, removed, removed_labels)
    held, prior_rows = pl.pallas_call(
        hold_kernel,
        out_shape=[shape(*own.shape), shape(K, width)],
        in_specs=[SMEM, VMEM],
        out_specs=[VMEM] * 2,
        compiler_params=params(24),
        name="hold",
    )(prior, own)
    edge_a = lax.ppermute(edge_a, "gy", pairs)
    edge_b = lax.ppermute(edge_b, "gy", others)
    last, (held, prior_rows) = gather(edge_b, (held, prior_rows))
    gathered = [held] + gather(own)[1:] + gather(edge_a) + last

    products = (design[:, :, None] * design[:, None, :]).reshape(K, K * K).T
    parts, rest = [], products
    for _ in range(3):
        part = lax.reduce_precision(rest, 8, 7)
        parts.append(part)
        rest = rest - part
    outer = jnp.concatenate([parts[a] for a, _ in SPLITS], axis=1).astype(jnp.bfloat16)

    field = shape(COUNTS[0], K, width)
    blocks, inverse, rhs = pl.pallas_call(
        setup_kernel,
        out_shape=[shape(width // 128, n, ROWS, 128) for n in (COUNTS[0], SLOTS)] + [field],
        in_specs=[VMEM] * (2 + len(gathered)),
        out_specs=[VMEM] * 3,
        scratch_shapes=[
            pltpu.VMEM((SLOTS, K, width), f32),
            pltpu.VMEM((width // 128, SLOTS // 2, len(SPLITS) * K, 256), jnp.bfloat16),
            pltpu.VMEM((width // 128, SLOTS - COUNTS[0], ROWS, 128), f32),
            pltpu.VMEM((4, K * K // 4, 8, 128), f32),
        ],
        compiler_params=params(24 if width == 128 else 60),
        name="setup",
    )(outer, prior_rows, *gathered)

    levels = [pltpu.VMEM((n, K, width), f32) for n in COUNTS[1:] * 2 + COUNTS[:-1] + COUNTS]
    tile = pltpu.VMEM((K * BLOCK, 128), f32)
    own_tile = shape(*beta.shape)
    whole = pltpu.VMEM((COUNTS[0], K, width), f32)
    edge = shape(COUNTS[0] // 4, K, width)

    def iterate(step, *operands, shapes, scratch=()):
        return pl.pallas_call(
            functools.partial(iterate_kernel, step),
            out_shape=shapes,
            in_specs=[VMEM] * (len(operands) + 3),
            out_specs=[VMEM] * len(shapes),
            scratch_shapes=list(scratch[:4]) + levels + list(scratch[4:]),
            compiler_params=params(24 if width == 128 else 60),
            name=f"iterate_{step}",
        )(prior_rows, blocks, inverse, *operands)

    def exchange(edge_a, edge_b):
        return lax.ppermute(edge_a, "gy", pairs), lax.ppermute(edge_b, "gy", others + [(0, cols - 1), (cols - 1, 0)])

    def total(parts):
        return lax.all_to_all(parts, "gy", 0, 0, tiled=True)

    residual, edges, image, earlier, sides, packed = rhs, (), (), (), (), ()
    for step in range(ITERS - 1):
        shapes = [field, field, edge, edge] + ([field] if step > 0 else [])
        z, az, *sent = iterate(step, residual, *edges, *image, shapes=shapes)
        edges, image, earlier = exchange(*sent[:2]), (az,), earlier + (z, az)
        if step > 0:
            residual = sent[2]
            fresh = [own_tile] * (2 if step == 1 else 1)
            side, *tiles = pl.pallas_call(
                functools.partial(side_kernel, step),
                out_shape=[shape(8, 128)] + fresh,
                in_specs=[VMEM] * len(earlier),
                out_specs=[VMEM] * (1 + len(fresh)),
                scratch_shapes=[tile],
                cost_estimate=pl.CostEstimate(flops=4_000_000, bytes_accessed=1_000_000, transcendentals=0),
                compiler_params=params(24 if width == 128 else 60),
                name=f"side_{step}",
            )(*earlier)
            sides, packed = sides + (side,), packed + tuple(tiles)
    parts, last_tile = iterate(
        ITERS - 1,
        residual,
        *edges,
        *image,
        *earlier,
        *sides,
        shapes=[shape(cols, 16, 128), own_tile],
        scratch=[whole] * 4 + [tile],
    )
    return pl.pallas_call(
        finish_kernel,
        out_shape=own_tile,
        in_specs=[VMEM] * (1 + ITERS),
        out_specs=VMEM,
        compiler_params=params(8),
        name="finish",
    )(total(parts), *packed, last_tile)


def solution(mesh):
    placed = (
        P(None, "gx", "gy"),
        P(),
        P(),
        P(None, "gx", "gy"),
        P(None, "gx", "gy"),
        P(None, "gx", "gy"),
    )
    return jax.shard_map(
        local, mesh=mesh, in_specs=placed, out_specs=P(None, "gx", "gy"), check_vma=False
    )
```
